32 devices in a mesh: ns: 8 (over y, x, core), ew: 4 (over z).
Axes of the slice: x: 2, y: 2, z: 4, core: 2. Of those that a mesh axis runs over, the one named last changes fastest.
Arguments:
- tokens: bfloat16 [64, 512, 512], P('ns', 'ew'), may hold values from -6 to 6
- conv_gain: float32 [512], replicated, may hold values from 0.1 to 1.9
- w_expand: bfloat16 [512, 2048], replicated, may hold values from -0.25 to 0.25
- dw_kernel: float32 [3, 3, 2048], replicated, may hold values from -2 to 2
- w_project: bfloat16 [2048, 512], replicated, may hold values from -0.375 to 0.375
- block_gain: float32 [512], replicated, may hold values from 0.1 to 1.9
- block_qkv: bfloat16 [512, 1536], replicated, may hold values from -2 to 2
- block_out: bfloat16 [512, 512], replicated, may hold values from -0.25 to 0.25
- grid_gain: float32 [512], replicated, may hold values from 0.1 to 1.9
- grid_qkv: bfloat16 [512, 1536], replicated, may hold values from -2 to 2
- grid_out: bfloat16 [512, 512], replicated, may hold values from -0.25 to 0.25
Outputs:
- block_output: bfloat16 [64, 512, 512], P('ns', 'ew')
The draws below stay inside these ranges and needn't reach their ends.
All inputs are finite; a program needn't handle non-finite values.
Results may differ from the reference program's by a relative error of at most 0.017.
Values may be sent and summed in bfloat16 or wider, within the bound.
No kernel may reach another device: no remote copies, remote signals or barrier semaphores. Data moves between devices by JAX's collectives and lax.ppermute only.
A program may use at most 128 MiB of HBM per device.

```python
import math
import jax
import jax.numpy as jnp
from jax import lax

C = 512
HEADS = 16
FFH = 2048
WINDOW = 8
ROWS = 64
COLS = 512


def projection_draw(base_key):
    key_query, key_key, key_value = jax.random.split(base_key, 3)
    queries = jax.random.normal(key_query, (C, C), jnp.float32) * (2.0 / math.sqrt(C))
    key_cols = jax.random.normal(key_key, (C, C), jnp.float32) * (2.0 / math.sqrt(C))
    value_cols = jax.random.normal(key_value, (C, C), jnp.float32) * (1.0 / math.sqrt(C))
    joined = jnp.concatenate([queries, key_cols, value_cols], axis=1)
    return jnp.clip(joined, -2.0, 2.0).astype(jnp.bfloat16)


def draw_block_qkv(key, part):
    return projection_draw(jax.random.fold_in(key, 11))


def draw_grid_qkv(key, part):
    return projection_draw(jax.random.fold_in(key, 23))


def block_levels(own_key, dims, shards, least, largest):
    gain = 1.0
    for axis_at, shards_of in shards:
        draws = jax.random.uniform(jax.random.fold_in(jax.random.fold_in(own_key, 6), axis_at), (shards_of,), jnp.float32, least / len(shards), largest / len(shards))
        gain = gain * jnp.repeat(jnp.exp(draws), dims[axis_at] // shards_of).reshape((-1,) + (1,) * (len(dims) - 1 - axis_at))
    return gain


def centred(rng, extent, scale, reach, shards=(), held_as=jnp.bfloat16):
    entries = scale * jax.random.normal(rng, extent, jnp.float32)
    if shards:
        entries = entries * block_levels(rng, extent, shards, -0.22, 0.18)
    return jnp.clip(entries, -reach, reach).astype(held_as)


def setup_inputs(seed: int = 0) -> dict:
    arg_keys = jax.random.split(jax.random.key(seed), 12)
    tokens = centred(arg_keys[0], (ROWS, COLS, C), 1.0, 6.0, ((0, 8), (1, 4)))
    conv_gain = jnp.clip(1.0 + 0.18 * jax.random.normal(arg_keys[1], (C,), jnp.float32), 0.1, 1.9)
    w_expand = centred(arg_keys[2], (C, FFH), C ** -0.5, 0.25)
    dw_kernel = centred(arg_keys[3], (3, 3, FFH), 9 ** -0.5, 2.0, (), jnp.float32)
    w_project = centred(arg_keys[4], (FFH, C), (FFH // 9) ** -0.5, 0.375)
    block_gain = jnp.clip(1.0 + 0.18 * jax.random.normal(arg_keys[5], (C,), jnp.float32), 0.1, 1.9)
    block_qkv = draw_block_qkv(jax.random.fold_in(arg_keys[11], 71), 0)
    block_out = centred(arg_keys[7], (C, C), C ** -0.5, 0.25)
    grid_gain = jnp.clip(1.0 + 0.18 * jax.random.normal(arg_keys[8], (C,), jnp.float32), 0.1, 1.9)
    grid_qkv = draw_grid_qkv(jax.random.fold_in(arg_keys[11], 71), 0)
    grid_out = centred(arg_keys[10], (C, C), C ** -0.5, 0.25)
    return dict(tokens=tokens, conv_gain=conv_gain, w_expand=w_expand, dw_kernel=dw_kernel, w_project=w_project, block_gain=block_gain, block_qkv=block_qkv, block_out=block_out, grid_gain=grid_gain, grid_qkv=grid_qkv, grid_out=grid_out)


def normalize(tokens, scale_gain):
    floats = tokens.astype(jnp.float32)
    center = floats - lax.optimization_barrier(jnp.mean(floats, axis=-1, keepdims=True))
    spread = lax.optimization_barrier(jnp.mean(center * center, axis=-1, keepdims=True))
    return (center * lax.rsqrt(spread + 1e-05) * scale_gain.astype(jnp.float32)).astype(jnp.bfloat16)

def expand_rows(tokens, scale_gain, w_expand):
    normed = normalize(tokens, scale_gain)
    flat_tokens = normed.reshape(-1, normed.shape[-1])
    hidden = jax.nn.gelu(jnp.dot(flat_tokens, w_expand, preferred_element_type=jnp.float32))
    return hidden.astype(jnp.bfloat16).reshape(tokens.shape[:-1] + (w_expand.shape[1],))

def depthwise(padded, dw_kernel, tile_rows, tile_cols):
    summed = jnp.zeros((tile_rows, tile_cols, padded.shape[-1]), jnp.float32)
    for offset_row in range(3):
        for offset_col in range(3):
            summed = summed + padded[offset_row:offset_row + tile_rows, offset_col:offset_col + tile_cols].astype(jnp.float32) * dw_kernel[offset_row, offset_col]
    return jax.nn.gelu(summed).astype(jnp.bfloat16)

def attend(tokens, scale_gain, w_qkv, w_out):
    layout = tokens.shape
    dim_p, dim_w, dim_q, dim_s, channels = layout
    head_dim = channels // HEADS
    normed = normalize(tokens, scale_gain).reshape(-1, channels)
    packed = jnp.dot(normed, w_qkv, preferred_element_type=jnp.float32).astype(jnp.bfloat16)
    packed = packed.reshape(dim_p, dim_w, dim_q, dim_s, 3, HEADS, head_dim)
    moved = jnp.transpose(packed, (4, 1, 3, 5, 0, 2, 6)).reshape(3, dim_w * dim_s, HEADS, dim_p * dim_q, head_dim)
    queries = moved[0].astype(jnp.float32)
    key_rows = moved[1].astype(jnp.float32)
    value_rows = moved[2].astype(jnp.float32)
    scores = jnp.einsum('nhqd,nhkd->nhqk', queries, key_rows) * head_dim ** (-0.5)
    weights = jax.nn.softmax(scores, axis=-1).astype(jnp.bfloat16)
    blended = jnp.einsum('nhqk,nhkd->nhqd', weights.astype(jnp.float32), value_rows).astype(jnp.bfloat16)
    blended = blended.reshape(dim_w, dim_s, HEADS, dim_p, dim_q, head_dim)
    blended = jnp.transpose(blended, (3, 0, 4, 1, 2, 5)).reshape(-1, channels)
    result = tokens.astype(jnp.float32).reshape(-1, channels) + jnp.dot(blended, w_out, preferred_element_type=jnp.float32)
    return result.astype(jnp.bfloat16).reshape(layout)

def reference(tokens, conv_gain, w_expand, dw_kernel, w_project, block_gain, block_qkv, block_out, grid_gain, grid_qkv, grid_out):
    rows_all, cols_all, channels = tokens.shape
    padded_rows = jnp.pad(tokens, ((1, 1), (0, 0), (0, 0)))

    def conv_band(band_index):
        row_start = band_index * WINDOW
        slab_rows = lax.dynamic_slice_in_dim(padded_rows, row_start, WINDOW + 2, 0)
        hidden = expand_rows(slab_rows, conv_gain, w_expand)
        position = row_start - 1 + jnp.arange(WINDOW + 2, dtype=jnp.int32)
        inside = (position >= 0) & (position < rows_all)
        hidden = jnp.where(inside[:, None, None], hidden, jnp.zeros_like(hidden))
        hidden = jnp.pad(hidden, ((0, 0), (1, 1), (0, 0)))
        active = depthwise(hidden, dw_kernel, WINDOW, cols_all)
        center = lax.dynamic_slice_in_dim(tokens, row_start, WINDOW, 0)
        update = jnp.dot(active.reshape(-1, active.shape[-1]), w_project, preferred_element_type=jnp.float32)
        return (center.astype(jnp.float32) + update.reshape(WINDOW, cols_all, channels)).astype(jnp.bfloat16)
    band_ids = jnp.arange(rows_all // WINDOW, dtype=jnp.int32)
    after_conv = lax.map(conv_band, band_ids).reshape(rows_all, cols_all, channels)

    def block_band(band_tokens):
        shaped = band_tokens.reshape(WINDOW, cols_all // WINDOW, WINDOW, 1, channels)
        return attend(shaped, block_gain, block_qkv, block_out).reshape(WINDOW, cols_all, channels)
    after_block = lax.map(block_band, after_conv.reshape(rows_all // WINDOW, WINDOW, cols_all, channels))
    after_block = after_block.reshape(rows_all, cols_all, channels)
    stride_rows = rows_all // WINDOW
    stride_cols = cols_all // WINDOW
    grouped = jnp.moveaxis(after_block.reshape(WINDOW, stride_rows, WINDOW, stride_cols, channels), 1, 0)

    def grid_row(row_tokens):
        shaped = row_tokens.reshape(WINDOW, 1, WINDOW, stride_cols, channels)
        return attend(shaped, grid_gain, grid_qkv, grid_out).reshape(WINDOW, WINDOW, stride_cols, channels)
    mixed_rows = lax.map(grid_row, grouped)
    return jnp.moveaxis(mixed_rows, 0, 1).reshape(rows_all, cols_all, channels)
```

```python
import functools
import math

import jax
import jax.numpy as jnp
from jax import lax
from jax.experimental import pallas as pl
from jax.experimental.pallas import tpu as pltpu
from jax.sharding import PartitionSpec as P

HEADS = 16
WINDOW = 8
FEATURES = 256
LANES = 128
GROUP = 4
VMEM_LIMIT = 56 * 1024 * 1024

NT = (((1,), (1,)), ((), ()))


def normalize(floats, scale_gain):
    center = floats - jnp.mean(floats, axis=-1, keepdims=True)
    spread = jnp.mean(center * center, axis=-1, keepdims=True)
    return center * lax.rsqrt(spread + 1e-05) * scale_gain


def gelu(v):
    inner = v * (math.sqrt(2 / math.pi) + (math.sqrt(2 / math.pi) * 0.044715) * (v * v))
    half = 0.5 * v
    return half + half * jnp.tanh(inner)


def tiles(value):
    return [value[:, t : t + LANES] for t in range(0, value.shape[1], LANES)]


def strided(ref, start, size, stride):
    return jnp.concatenate([ref[t, pl.ds(start, size, stride=stride), :] for t in range(ref.shape[0])], axis=1)


def conv_kernel(
    slot_of, x_ref, edge_ref, side_ref, gain_ref, w1_ref, dw_ref, w2_ref, out_ref, n_ref, tmp_ref, e_ref, acc_ref
):
    step = pl.program_id(0)
    rows, cols, _ = x_ref.shape
    strips = cols // WINDOW
    features = w1_ref.shape[1]
    side_count = side_ref.shape[0] // 2
    gain = gain_ref[...]

    @pl.when(step == 0)
    def _():
        def place(slot, block):
            for t, part in enumerate(tiles(normalize(block.astype(jnp.float32), gain))):
                tmp_ref[t] = part
            for b in range(WINDOW):
                start = pl.multiple_of(slot * cols + b * strips, strips)
                n_ref[pl.ds(start, strips), :] = strided(tmp_ref, b, strips, WINDOW).astype(jnp.bfloat16)

        @pl.loop(0, rows)
        def _(i):
            place(i + 1, x_ref[i])

        place(0, edge_ref[0])
        place(rows + 1, edge_ref[1])
        n_ref[pl.ds((rows + 2) * cols, 2 * side_count), :] = normalize(
            side_ref[...].astype(jnp.float32), gain
        ).astype(jnp.bfloat16)
        acc_ref[...] = jnp.zeros_like(acc_ref)

    w1 = w1_ref[...]
    w2 = w2_ref[...]
    taps = [[dw_ref[3 * a + b : 3 * a + b + 1, :].astype(jnp.bfloat16) for b in range(3)] for a in range(3)]
    sides = gelu(
        jnp.dot(n_ref[pl.ds((rows + 2) * cols, 2 * side_count), :], w1, preferred_element_type=jnp.float32)
    )
    place_in_strip = lax.broadcasted_iota(jnp.int32, (strips, features), 0)

    def expand(i):
        hidden = gelu(
            jnp.dot(n_ref[pl.ds(i * cols, cols), :], w1, preferred_element_type=jnp.float32).astype(jnp.bfloat16)
        )
        e_ref[i, 1 : WINDOW + 1] = hidden.reshape(WINDOW, strips, features)
        last = pltpu.roll(hidden[(WINDOW - 1) * strips :].astype(jnp.float32), 1, axis=0)
        first = pltpu.roll(hidden[:strips].astype(jnp.float32), strips - 1, axis=0)
        low = jnp.where(place_in_strip == 0, sides[i : i + 1], last)
        high = jnp.where(place_in_strip == strips - 1, sides[side_count + i : side_count + i + 1], first)
        e_ref[i, 0] = low.astype(jnp.bfloat16)
        e_ref[i, WINDOW + 1] = high.astype(jnp.bfloat16)

    def contract(i):
        pieces = []
        for b in range(WINDOW):
            parts = []
            for da in range(3):
                t = [e_ref[i + da, b + db] * taps[da][db] for db in range(3)]
                parts.append(t[0] + t[1] + t[2])
            pieces.append(gelu(parts[0] + parts[1] + parts[2]))
        active = jnp.concatenate(pieces, axis=0)
        for t, part in enumerate(tiles(jnp.dot(active, w2, preferred_element_type=jnp.float32))):
            acc_ref[t, i * cols : (i + 1) * cols, :] += part

    for i in range(rows + 2):
        expand(i)
        if i >= 2:
            contract(i - 2)

    @pl.when(step == pl.num_programs(0) - 1)
    def _():
        for pair in range(strips // 2):
            tokens = x_ref[:, pair * 2 * WINDOW : (pair + 1) * 2 * WINDOW, :].astype(jnp.float32)
            for odd in range(2):
                window = 2 * pair + odd
                own = tokens[:, odd * WINDOW : (odd + 1) * WINDOW, :].reshape(rows * WINDOW, -1)
                summed = own + strided(acc_ref, window, rows * WINDOW, strips)
                out_ref[slot_of(window)] = summed.astype(jnp.bfloat16)


def conv_block(tokens, edge, side, gain, w_expand, dw_kernel, w_project, slot_of):
    rows, cols, channels = tokens.shape
    width = w_expand.shape[1]
    features = min(FEATURES, width)
    strips = cols // WINDOW
    whole = lambda *shape: pl.BlockSpec(shape, lambda f: (0,) * len(shape))
    return pl.pallas_call(
        functools.partial(conv_kernel, slot_of),
        grid=(width // features,),
        out_shape=jax.ShapeDtypeStruct((strips, rows * WINDOW, channels), jnp.bfloat16),
        in_specs=[
            whole(*tokens.shape),
            whole(*edge.shape),
            whole(*side.shape),
            whole(1, channels),
            pl.BlockSpec((channels, features), lambda f: (0, f)),
            pl.BlockSpec((9, features), lambda f: (0, f)),
            pl.BlockSpec((features, channels), lambda f: (f, 0)),
        ],
        out_specs=whole(strips, rows * WINDOW, channels),
        scratch_shapes=[
            pltpu.VMEM(((rows + 2) * cols + side.shape[0], channels), jnp.bfloat16),
            pltpu.VMEM((channels // LANES, cols, LANES), jnp.float32),
            pltpu.VMEM((rows + 2, WINDOW + 2, strips, features), jnp.bfloat16),
            pltpu.VMEM((channels // LANES, rows * cols, LANES), jnp.float32),
        ],
        compiler_params=pltpu.CompilerParams(
            dimension_semantics=("arbitrary",), vmem_limit_bytes=VMEM_LIMIT
        ),
        cost_estimate=pl.CostEstimate(
            flops=4 * rows * cols * channels * width,
            bytes_accessed=4 * channels * width + 4 * rows * cols * channels,
            transcendentals=2 * rows * cols * width,
        ),
        name="conv_block",
    )(
        tokens,
        edge,
        side,
        gain.reshape(1, channels),
        w_expand,
        dw_kernel.reshape(9, width),
        w_project,
    )


def attend_windows(x, gain, wqk, wvt, wout):
    tokens, channels = x.shape
    head_dim = channels // HEADS
    group = LANES // head_dim
    size = WINDOW * WINDOW
    scale = math.log2(math.e) / math.sqrt(head_dim)
    normed = normalize(x, gain).astype(jnp.bfloat16)
    queries = (jnp.dot(normed, wqk[:, :channels], preferred_element_type=jnp.float32) * scale).astype(jnp.bfloat16)
    keys = jnp.dot(normed, wqk[:, channels : 2 * channels], preferred_element_type=jnp.float32).astype(jnp.bfloat16)
    values = lax.dot_general(wvt, normed, NT, preferred_element_type=jnp.float32).astype(jnp.bfloat16)
    lane = lax.broadcasted_iota(jnp.int32, (size, LANES), 1)
    head_lanes = [lane // head_dim == h for h in range(group)]
    half = lax.broadcasted_iota(jnp.int32, (LANES, 2 * size), 1) // size
    block_row = lax.broadcasted_iota(jnp.int32, (2 * LANES, group * size), 0) % LANES // head_dim
    block_col = lax.broadcasted_iota(jnp.int32, (2 * LANES, group * size), 1) // size
    own_block = block_row == block_col
    pick = (
        lax.broadcasted_iota(jnp.int32, (size, group * size), 0)
        == lax.broadcasted_iota(jnp.int32, (size, group * size), 1) % size
    ).astype(jnp.bfloat16)
    zero = jnp.zeros((), jnp.bfloat16)
    blended = []
    for pair in range(tokens // (2 * size)):
        parts = []
        for g in range(channels // LANES):
            weights = []
            for odd in range(2):
                at = (2 * pair + odd) * size
                q = queries[at : at + size, g * LANES : (g + 1) * LANES]
                k = keys[at : at + size, g * LANES : (g + 1) * LANES]
                q_heads = jnp.concatenate([jnp.where(m, q, zero) for m in head_lanes], axis=0)
                scores = lax.dot_general(k, q_heads, NT, preferred_element_type=jnp.float32)
                raised = jnp.exp2(scores - jnp.max(scores, axis=0, keepdims=True))
                weights.append(
                    (raised * (1.0 / jnp.sum(raised, axis=0, keepdims=True))).astype(jnp.bfloat16)
                )
            v = values[g * LANES : (g + 1) * LANES, pair * 2 * size : (pair + 1) * 2 * size]
            v_halves = jnp.concatenate([jnp.where(half == 0, v, zero), jnp.where(half == 1, v, zero)], axis=0)
            mixed = jnp.dot(v_halves, jnp.concatenate(weights, axis=0), preferred_element_type=jnp.float32)
            mixed = jnp.where(own_block, mixed, 0.0).astype(jnp.bfloat16)
            parts.append(lax.dot_general(pick, mixed, NT, preferred_element_type=jnp.float32).astype(jnp.bfloat16))
        for odd in range(2):
            blended.append(
                jnp.concatenate([part[:, odd * LANES : (odd + 1) * LANES] for part in parts], axis=1)
            )
    return x + jnp.dot(jnp.concatenate(blended, axis=0), wout, preferred_element_type=jnp.float32)


def window_kernel(x_ref, gain_ref, wqk_ref, wvt_ref, wout_ref, out_ref):
    count, size, channels = x_ref.shape
    _, places, shares, side, _ = out_ref.shape
    x = x_ref[...].astype(jnp.float32).reshape(count * size, channels)
    result = attend_windows(x, gain_ref[...], wqk_ref, wvt_ref[...], wout_ref[...]).astype(jnp.bfloat16)
    result = result.reshape(places, shares, size // side, side, channels)
    for j in range(places):
        for share in range(shares):
            out_ref[:, j, share] = result[j, share]


def attention_call(kernel, name, grid, x, x_spec, gain, weights, out_shape, out_spec, scratch):
    channels = x.shape[-1]
    tokens = x.size // channels
    whole = lambda array: pl.BlockSpec(array.shape, lambda step: (0,) * array.ndim)
    gain = gain.reshape(1, channels)
    return pl.pallas_call(
        kernel,
        grid=(grid,),
        out_shape=jax.ShapeDtypeStruct(out_shape, jnp.bfloat16),
        in_specs=[x_spec, whole(gain)] + [whole(w) for w in weights],
        out_specs=out_spec,
        scratch_shapes=scratch,
        compiler_params=pltpu.CompilerParams(
            dimension_semantics=("arbitrary",), vmem_limit_bytes=VMEM_LIMIT
        ),
        cost_estimate=pl.CostEstimate(
            flops=16 * tokens * channels * channels,
            bytes_accessed=8 * channels * channels + 4 * tokens * channels,
            transcendentals=HEADS * tokens * WINDOW * WINDOW,
        ),
        name=name,
    )(x, gain, *weights)


def window_attention(x, chunk, chunks, shares, gain, weights):
    windows, size, channels = x.shape
    per_chunk = windows // chunks
    block = min(GROUP, per_chunk)
    steps = per_chunk // block
    return attention_call(
        window_kernel,
        "window_attention",
        steps,
        x,
        pl.BlockSpec((block, size, channels), lambda step: (chunk * steps + step, 0, 0)),
        gain,
        weights,
        (size // WINDOW, per_chunk // shares, shares, WINDOW, channels),
        pl.BlockSpec((size // WINDOW, block // shares, shares, WINDOW, channels), lambda step: (0, step, 0, 0, 0)),
        [],
    )


def grid_kernel(x_ref, gain_ref, wqk_ref, wvt_ref, wout_ref, out_ref, floats_ref):
    step = pl.program_id(0)
    tokens, channels = x_ref.shape
    size = WINDOW * WINDOW
    windows = tokens // size
    block = windows // pl.num_programs(0)

    @pl.when(step == 0)
    def _():
        for t, part in enumerate(tiles(x_ref[...])):
            floats_ref[t] = part.astype(jnp.float32)

    first = step * block
    x = jnp.concatenate([strided(floats_ref, first + w, size, windows) for w in range(block)], axis=0)
    result = attend_windows(x, gain_ref[...], wqk_ref, wvt_ref[...], wout_ref[...])
    for t, part in enumerate(tiles(result)):
        for w in range(block):
            floats_ref[t, pl.ds(first + w, size, stride=windows), :] = part[w * size : (w + 1) * size]

    @pl.when(step == pl.num_programs(0) - 1)
    def _():
        for t in range(floats_ref.shape[0]):
            out_ref[:, t * LANES : (t + 1) * LANES] = floats_ref[t].astype(jnp.bfloat16)


def grid_attention(x, gain, weights):
    tokens, channels = x.shape
    windows = tokens // (WINDOW * WINDOW)
    spec = pl.BlockSpec((tokens, channels), lambda step: (0, 0))
    return attention_call(
        grid_kernel,
        "grid_attention",
        windows // min(GROUP, windows),
        x,
        spec,
        gain,
        weights,
        (tokens, channels),
        spec,
        [pltpu.VMEM((channels // LANES, tokens, LANES), jnp.float32)],
    )


def halo(tokens):
    rows, cols, channels = tokens.shape
    bands = [(i, i + 1) for i in range(lax.axis_size("ns") - 1)]
    strips = [(i, i + 1) for i in range(lax.axis_size("ew") - 1)]
    back = lambda pairs: [(target, source) for source, target in pairs]
    north = lax.ppermute(tokens[rows - 1], "ns", bands)
    south = lax.ppermute(tokens[0], "ns", back(bands))
    west = lax.ppermute(
        jnp.concatenate([north[None, cols - 1], tokens[:, cols - 1], south[None, cols - 1]]), "ew", strips
    )
    east = lax.ppermute(jnp.concatenate([north[None, 0], tokens[:, 0], south[None, 0]]), "ew", back(strips))
    pad = ((0, -(rows + 2) % 16), (0, 0))
    return jnp.stack([north, south]), jnp.concatenate([jnp.pad(west, pad), jnp.pad(east, pad)])


def exchange(x):
    bands, strips = lax.axis_size("ns"), lax.axis_size("ew")
    if bands == WINDOW:
        return lax.all_to_all(x, ("ns", "ew"), 0, 0, tiled=True)
    inner = bands // WINDOW
    groups = [[a * inner + p for a in range(WINDOW)] for p in range(inner)]
    shape = x.shape
    x = x.reshape(WINDOW, strips, *shape[1:])
    x = lax.all_to_all(x, "ns", 0, 0, axis_index_groups=groups, tiled=True)
    x = lax.all_to_all(x, "ew", 1, 1, tiled=True)
    return x.reshape(shape)


def attention_weights(w_qkv, w_out):
    channels = w_out.shape[0]
    return w_qkv[:, : 2 * channels], w_qkv[:, 2 * channels :].T, w_out


def on_device(
    tokens,
    conv_gain,
    w_expand,
    dw_kernel,
    w_project,
    block_gain,
    block_qkv,
    block_out,
    grid_gain,
    grid_qkv,
    grid_out,
):
    rows, cols, channels = tokens.shape
    shares = WINDOW // lax.axis_size("ew")
    group = WINDOW * lax.axis_size("ew")
    across = cols // shares // WINDOW
    places = group // rows
    chunks = across // places

    def slot_of(window):
        share, at = divmod(window, across)
        chunk, place = divmod(at, places)
        return (chunk * places + place) * shares + share

    edge, side = halo(tokens)
    after_conv = conv_block(tokens, edge, side, conv_gain, w_expand, dw_kernel, w_project, slot_of)
    block_weights = attention_weights(block_qkv, block_out)
    grid_weights = attention_weights(grid_qkv, grid_out)
    sent = []
    for chunk in range(chunks):
        x = window_attention(after_conv, chunk, chunks, shares, block_gain, block_weights)
        sent.append(exchange(x.reshape(group, shares * WINDOW, channels)))
    returned = []
    for x in sent:
        y = grid_attention(x.reshape(-1, channels), grid_gain, grid_weights)
        returned.append(exchange(y.reshape(group, shares * WINDOW, channels)))
    pieces = [y.reshape(rows, places, shares, WINDOW, channels) for y in returned]
    joined = jnp.stack(pieces)
    return jnp.transpose(joined, (1, 3, 0, 2, 4, 5)).reshape(rows, cols, channels)


def solution(mesh):
    in_specs = (P("ns", "ew", None), P(), P(), P(), P(), P(), P(), P(), P(), P(), P())
    out_specs = P("ns", "ew", None)
    return jax.shard_map(
        on_device, mesh=mesh, in_specs=in_specs, out_specs=out_specs, check_vma=False
    )
```

```python
import functools
import math

import jax
import jax.numpy as jnp
from jax import lax
from jax.experimental import pallas as pl
from jax.experimental.pallas import tpu as pltpu
from jax.sharding import PartitionSpec as P

HEADS = 16
WINDOW = 8
FEATURES = 1024
LANES = 128
GROUP = 8
SENDS = 1
MIB = 1024 * 1024

NT = (((1,), (1,)), ((), ()))


def normalize(floats, scale_gain):
    center = floats - jnp.mean(floats, axis=-1, keepdims=True)
    spread = jnp.mean(center * center, axis=-1, keepdims=True)
    return center * lax.rsqrt(spread + 1e-05) * scale_gain


def gelu(v):
    inner = v * (math.sqrt(2 / math.pi) + (math.sqrt(2 / math.pi) * 0.044715) * (v * v))
    half = 0.5 * v
    return half + half * jnp.tanh(inner)


def tiles(value):
    return [value[:, t : t + LANES] for t in range(0, value.shape[1], LANES)]


def strided(ref, start, size, stride):
    return jnp.concatenate([ref[t, pl.ds(start, size, stride=stride), :] for t in range(ref.shape[0])], axis=1)


def conv_kernel(
    slot_of, x_ref, ns0_ref, ns1_ref, ew0_ref, ew1_ref, gain_ref, w1_ref, dw_ref, w2_ref, out_ref,
    n_ref, tmp_ref, e_ref, acc_ref
):
    step = pl.program_id(0)
    rows, cols, _ = x_ref.shape
    strips = cols // WINDOW
    features = w1_ref.shape[1]
    side_rows = ew0_ref.shape[0]
    side_count = side_rows + -side_rows % 16
    gain = gain_ref[...]

    @pl.when(step == 0)
    def _():
        def place(slot, block):
            for t, part in enumerate(tiles(normalize(block, gain))):
                tmp_ref[t] = part
            for b in range(WINDOW):
                start = slot * cols + b * strips
                n_ref[start : start + strips, :] = strided(tmp_ref, b, strips, WINDOW).astype(jnp.bfloat16)

        def sorted_pair(first_ref, second_ref, axis):
            first, second = first_ref[...].astype(jnp.float32), second_ref[...].astype(jnp.float32)
            even = lax.rem(lax.axis_index(axis), 2) == 0
            return jnp.where(even, second, first), jnp.where(even, first, second)

        for i in range(rows):
            place(i + 1, x_ref[i].astype(jnp.float32))
        north, south = sorted_pair(ns0_ref, ns1_ref, "ns")
        place(0, north)
        place(rows + 1, south)
        pad = jnp.zeros((side_count - side_rows, x_ref.shape[2]), jnp.float32)
        for k, block in enumerate(sorted_pair(ew0_ref, ew1_ref, "ew")):
            start = (rows + 2) * cols + k * side_count
            n_ref[start : start + side_count, :] = normalize(
                jnp.concatenate([block, pad], axis=0), gain
            ).astype(jnp.bfloat16)
        acc_ref[...] = jnp.zeros_like(acc_ref)

    w1 = w1_ref[...]
    w2 = w2_ref[...]
    taps = [[dw_ref[3 * a + b : 3 * a + b + 1, :].astype(jnp.bfloat16) for b in range(3)] for a in range(3)]
    sides = gelu(
        jnp.dot(n_ref[pl.ds((rows + 2) * cols, 2 * side_count), :], w1, preferred_element_type=jnp.float32)
    )
    place_in_strip = lax.broadcasted_iota(jnp.int32, (strips, features), 0)

    def expand(i):
        hidden = gelu(
            jnp.dot(n_ref[pl.ds(i * cols, cols), :], w1, preferred_element_type=jnp.float32).astype(jnp.bfloat16)
        )
        e_ref[i, 1 : WINDOW + 1] = hidden.reshape(WINDOW, strips, features)
        last = pltpu.roll(hidden[(WINDOW - 1) * strips :].astype(jnp.float32), 1, axis=0)
        first = pltpu.roll(hidden[:strips].astype(jnp.float32), strips - 1, axis=0)
        low = jnp.where(place_in_strip == 0, sides[i : i + 1], last)
        high = jnp.where(place_in_strip == strips - 1, sides[side_count + i : side_count + i + 1], first)
        e_ref[i, 0] = low.astype(jnp.bfloat16)
        e_ref[i, WINDOW + 1] = high.astype(jnp.bfloat16)

    def contract(i):
        pieces = []
        for b in range(WINDOW):
            parts = []
            for da in range(3):
                t = [e_ref[i + da, b + db] * taps[da][db] for db in range(3)]
                parts.append(t[0] + t[1] + t[2])
            pieces.append(gelu(parts[0] + parts[1] + parts[2]))
        active = jnp.concatenate(pieces, axis=0)
        for t, part in enumerate(tiles(jnp.dot(active, w2, preferred_element_type=jnp.float32))):
            acc_ref[t, i * cols : (i + 1) * cols, :] += part

    for i in range(rows + 2):
        expand(i)
    for i in range(rows):
        contract(i)

    @pl.when(step == pl.num_programs(0) - 1)
    def _():
        for pair in range(strips // 2):
            tokens = x_ref[:, pair * 2 * WINDOW : (pair + 1) * 2 * WINDOW, :].astype(jnp.float32)
            for odd in range(2):
                window = 2 * pair + odd
                own = tokens[:, odd * WINDOW : (odd + 1) * WINDOW, :].reshape(rows * WINDOW, -1)
                summed = own + strided(acc_ref, window, rows * WINDOW, strips)
                out_ref[slot_of(window)] = summed.astype(jnp.bfloat16)


def conv_block(tokens, swaps, gain, w_expand, dw_kernel, w_project, slot_of):
    rows, cols, channels = tokens.shape
    width = w_expand.shape[1]
    features = min(FEATURES, width)
    strips = cols // WINDOW
    side_count = swaps[2].shape[0] + -swaps[2].shape[0] % 16
    whole = lambda *shape: pl.BlockSpec(shape, lambda f: (0,) * len(shape))
    return pl.pallas_call(
        functools.partial(conv_kernel, slot_of),
        grid=(width // features,),
        out_shape=jax.ShapeDtypeStruct((strips, rows * WINDOW, channels), jnp.bfloat16),
        in_specs=[
            whole(*tokens.shape),
            *[whole(*swap.shape) for swap in swaps],
            whole(1, channels),
            pl.BlockSpec((channels, features), lambda f: (0, f)),
            pl.BlockSpec((9, features), lambda f: (0, f)),
            pl.BlockSpec((features, channels), lambda f: (f, 0)),
        ],
        out_specs=whole(strips, rows * WINDOW, channels),
        scratch_shapes=[
            pltpu.VMEM(((rows + 2) * cols + 2 * side_count, channels), jnp.bfloat16),
            pltpu.VMEM((channels // LANES, cols, LANES), jnp.float32),
            pltpu.VMEM((rows + 2, WINDOW + 2, strips, features), jnp.bfloat16),
            pltpu.VMEM((channels // LANES, rows * cols, LANES), jnp.float32),
        ],
        compiler_params=pltpu.CompilerParams(
            dimension_semantics=("arbitrary",), vmem_limit_bytes=40 * MIB
        ),
        cost_estimate=pl.CostEstimate(
            flops=4 * rows * cols * channels * width,
            bytes_accessed=4 * channels * width + 4 * rows * cols * channels,
            transcendentals=2 * rows * cols * width,
        ),
        name="conv_block",
    )(
        tokens,
        *swaps,
        gain.reshape(1, channels),
        w_expand,
        dw_kernel.reshape(9, width),
        w_project,
    )


def attend_windows(x, gain, wqkv_ref, wout_ref):
    tokens, channels = x.shape
    head_dim = channels // HEADS
    group = LANES // head_dim
    size = WINDOW * WINDOW
    two = 2 * head_dim
    pairs, groups = tokens // (2 * size), channels // LANES
    units = [(p, g) for p in range(pairs) for g in range(groups)]
    scale = math.log2(math.e) / math.sqrt(head_dim)
    normed = normalize(x, gain).astype(jnp.bfloat16)

    def project(first):
        return jnp.dot(normed, wqkv_ref[:, first : first + channels], preferred_element_type=jnp.float32)

    queries = (project(0) * scale).astype(jnp.bfloat16)
    keys = project(channels).astype(jnp.bfloat16)
    values = lax.dot_general(
        wqkv_ref[:, 2 * channels :].T, normed, NT, preferred_element_type=jnp.float32
    ).astype(jnp.bfloat16)
    lane = lax.broadcasted_iota(jnp.int32, (1, LANES), 1)
    head_lanes = [(lane // head_dim == h).astype(jnp.float32).astype(jnp.bfloat16) for h in range(group)]
    halves = [(lane // size == h).astype(jnp.float32).astype(jnp.bfloat16) for h in range(2)]
    pick = (
        (
            lax.broadcasted_iota(jnp.int32, (size, 2 * size), 0)
            == lax.broadcasted_iota(jnp.int32, (size, 2 * size), 1) % size
        )
        .astype(jnp.float32)
        .astype(jnp.bfloat16)
    )
    scores = {}
    for p, g in units:
        for odd in range(2):
            at = (2 * p + odd) * size
            q = queries[at : at + size, g * LANES : (g + 1) * LANES]
            k = keys[at : at + size, g * LANES : (g + 1) * LANES]
            q_heads = jnp.concatenate([q * m for m in head_lanes], axis=0)
            scores[p, g, odd] = lax.dot_general(k, q_heads, NT, preferred_element_type=jnp.float32)
    weights = {}
    for unit, s in scores.items():
        raised = jnp.exp2(s - jnp.max(s, axis=0, keepdims=True))
        weights[unit] = (raised * (1.0 / jnp.sum(raised, axis=0, keepdims=True))).astype(jnp.bfloat16)
    mixed = {}
    for p, g in units:
        both = jnp.concatenate([weights[p, g, 0], weights[p, g, 1]], axis=0)
        for t in range(group // 2):
            at = g * LANES + t * two
            v = values[at : at + two, p * 2 * size : (p + 1) * 2 * size]
            v_halves = jnp.concatenate([v * m for m in halves], axis=0)
            mixed[p, g, t] = jnp.dot(
                v_halves, both[:, t * 2 * size : (t + 1) * 2 * size], preferred_element_type=jnp.float32
            ).astype(jnp.bfloat16)
    parts = {}
    for p, g in units:
        own = [
            mixed[p, g, t][odd * two + h * head_dim : odd * two + (h + 1) * head_dim] * halves[h]
            for odd in range(2)
            for t in range(group // 2)
            for h in range(2)
        ]
        parts[p, g] = lax.dot_general(
            pick, jnp.concatenate(own, axis=0), NT, preferred_element_type=jnp.float32
        ).astype(jnp.bfloat16)
    blended = [
        jnp.concatenate([parts[p, g][:, odd * LANES : (odd + 1) * LANES] for g in range(groups)], axis=1)
        for p in range(pairs)
        for odd in range(2)
    ]
    return x + jnp.dot(jnp.concatenate(blended, axis=0), wout_ref[...], preferred_element_type=jnp.float32)


def window_kernel(x_ref, gain_ref, wqkv_ref, wout_ref, out_ref):
    count, size, channels = x_ref.shape
    _, places, shares, parts, side, _ = out_ref.shape
    x = x_ref[...].astype(jnp.float32).reshape(count * size, channels)
    result = attend_windows(x, gain_ref[...], wqkv_ref, wout_ref).astype(jnp.bfloat16)
    result = result.reshape(places, shares, parts, size // side, side, channels)
    for j in range(places):
        for share in range(shares):
            for part in range(parts):
                out_ref[:, j, share, part] = result[j, share, part]


def attention_call(kernel, name, grid, x, x_spec, gain, weights, out_shape, out_spec, scratch):
    channels = x.shape[-1]
    tokens = x.size // channels
    whole = lambda array: pl.BlockSpec(array.shape, lambda step: (0,) * array.ndim)
    gain = gain.reshape(1, channels)
    return pl.pallas_call(
        kernel,
        grid=(grid,),
        out_shape=jax.ShapeDtypeStruct(out_shape, jnp.bfloat16),
        in_specs=[x_spec, whole(gain)] + [whole(w) for w in weights],
        out_specs=out_spec,
        scratch_shapes=scratch,
        compiler_params=pltpu.CompilerParams(
            dimension_semantics=("arbitrary",), vmem_limit_bytes=24 * MIB
        ),
        cost_estimate=pl.CostEstimate(
            flops=16 * tokens * channels * channels,
            bytes_accessed=8 * channels * channels + 4 * tokens * channels,
            transcendentals=HEADS * tokens * WINDOW * WINDOW,
        ),
        name=name,
    )(x, gain, *weights)


def window_attention(x, send, sends, places, shares, gain, weights):
    windows, size, channels = x.shape
    per_send = windows // sends
    parts = per_send // (places * shares)
    block_places = max(1, min(places, GROUP // (shares * parts)))
    block = block_places * shares * parts
    steps = per_send // block
    return attention_call(
        window_kernel,
        "window_attention",
        steps,
        x,
        pl.BlockSpec((block, size, channels), lambda step: (send * steps + step, 0, 0)),
        gain,
        weights,
        (size // WINDOW, places, shares, parts, WINDOW, channels),
        pl.BlockSpec(
            (size // WINDOW, block_places, shares, parts, WINDOW, channels), lambda step: (0, step, 0, 0, 0, 0)
        ),
        [],
    )


def grid_kernel(x_ref, gain_ref, wqkv_ref, wout_ref, out_ref, floats_ref):
    step = pl.program_id(0)
    tokens, channels = x_ref.shape
    size = WINDOW * WINDOW
    windows = tokens // size
    block = windows // pl.num_programs(0)

    @pl.when(step == 0)
    def _():
        for t, part in enumerate(tiles(x_ref[...])):
            floats_ref[t] = part.astype(jnp.float32)

    first = step * block
    x = jnp.concatenate([strided(floats_ref, first + w, size, windows) for w in range(block)], axis=0)
    result = attend_windows(x, gain_ref[...], wqkv_ref, wout_ref)
    for t, part in enumerate(tiles(result)):
        for w in range(block):
            floats_ref[t, pl.ds(first + w, size, stride=windows), :] = part[w * size : (w + 1) * size]

    @pl.when(step == pl.num_programs(0) - 1)
    def _():
        for t in range(floats_ref.shape[0]):
            out_ref[:, t * LANES : (t + 1) * LANES] = floats_ref[t].astype(jnp.bfloat16)


def grid_attention(x, gain, weights):
    tokens, channels = x.shape
    windows = tokens // (WINDOW * WINDOW)
    spec = pl.BlockSpec((tokens, channels), lambda step: (0, 0))
    return attention_call(
        grid_kernel,
        "grid_attention",
        windows // min(GROUP, windows),
        x,
        spec,
        gain,
        weights,
        (tokens, channels),
        spec,
        [pltpu.VMEM((channels // LANES, tokens, LANES), jnp.float32)],
    )


def swap(low_edge, high_edge, axis, first):
    pairs = [(a, a + 1) for a in range(first, lax.axis_size(axis) - 1, 2)]
    lower = lax.rem(lax.axis_index(axis), 2) == first
    return lax.ppermute(
        jnp.where(lower, high_edge, low_edge), axis, pairs + [(target, source) for source, target in pairs]
    )


def halo(tokens):
    rows, cols, _ = tokens.shape
    ns0, ns1 = [swap(tokens[0], tokens[rows - 1], "ns", first) for first in range(2)]
    even = lax.rem(lax.axis_index("ns"), 2) == 0

    def column(c):
        north, south = jnp.where(even, ns1[c], ns0[c]), jnp.where(even, ns0[c], ns1[c])
        return jnp.concatenate([north[None], tokens[:, c], south[None]])

    ew0, ew1 = [swap(column(0), column(cols - 1), "ew", first) for first in range(2)]
    return ns0, ns1, ew0, ew1


def exchange(x):
    bands, strips = lax.axis_size("ns"), lax.axis_size("ew")
    if bands == WINDOW:
        return lax.all_to_all(x, ("ns", "ew"), 0, 0, tiled=True)
    inner = bands // WINDOW
    groups = [[a * inner + p for a in range(WINDOW)] for p in range(inner)]
    shape = x.shape
    x = x.reshape(WINDOW, strips, *shape[1:])
    x = lax.all_to_all(x, "ns", 0, 0, axis_index_groups=groups, tiled=True)
    x = lax.all_to_all(x, "ew", 1, 1, tiled=True)
    return x.reshape(shape)


def on_device(
    tokens,
    conv_gain,
    w_expand,
    dw_kernel,
    w_project,
    block_gain,
    block_qkv,
    block_out,
    grid_gain,
    grid_qkv,
    grid_out,
):
    rows, cols, channels = tokens.shape
    shares = WINDOW // lax.axis_size("ew")
    group = WINDOW * lax.axis_size("ew")
    across = cols // shares // WINDOW
    places = group // rows
    parts = across // places
    sends = min(SENDS, parts)
    per_send = parts // sends

    def slot_of(window):
        share, at = divmod(window, across)
        part, place = divmod(at, places)
        send, part = divmod(part, per_send)
        return ((send * places + place) * shares + share) * per_send + part

    after_conv = conv_block(tokens, halo(tokens), conv_gain, w_expand, dw_kernel, w_project, slot_of)
    sent = []
    for send in range(sends):
        x = window_attention(after_conv, send, sends, places, shares, block_gain, (block_qkv, block_out))
        sent.append(exchange(x.reshape(group, -1, channels)))
    returned = []
    for x in sent:
        y = grid_attention(x.reshape(-1, channels), grid_gain, (grid_qkv, grid_out))
        returned.append(exchange(y.reshape(group, -1, channels)))
    pieces = [y.reshape(rows, places, shares, per_send, WINDOW, channels) for y in returned]
    return jnp.transpose(jnp.stack(pieces), (1, 3, 0, 4, 2, 5, 6)).reshape(rows, cols, channels)


def solution(mesh):
    in_specs = (P("ns", "ew", None), P(), P(), P(), P(), P(), P(), P(), P(), P(), P())
    out_specs = P("ns", "ew", None)
    return jax.shard_map(
        on_device, mesh=mesh, in_specs=in_specs, out_specs=out_specs, check_vma=False
    )
```

```python
import functools
import math

import jax
import jax.numpy as jnp
from jax import lax
from jax.experimental import pallas as pl
from jax.experimental.pallas import tpu as pltpu
from jax.sharding import PartitionSpec as P

HEADS = 16
WINDOW = 8
EXPAND = 512
FEATURES = 1024
LANES = 128
GROUP = 8
MIB = 1024 * 1024

NT = (((1,), (1,)), ((), ()))


def normalize(floats, scale_gain):
    center = floats - jnp.mean(floats, axis=-1, keepdims=True)
    spread = jnp.mean(center * center, axis=-1, keepdims=True)
    return center * lax.rsqrt(spread + 1e-05) * scale_gain


def gelu(v):
    inner = v * (math.sqrt(2 / math.pi) + (math.sqrt(2 / math.pi) * 0.044715) * (v * v))
    half = 0.5 * v
    return half + half * jnp.tanh(inner)


def tiles(value):
    return [value[:, t : t + LANES] for t in range(0, value.shape[1], LANES)]


def strided(ref, start, size, stride):
    return jnp.concatenate([ref[t, pl.ds(start, size, stride=stride), :] for t in range(ref.shape[0])], axis=1)


def by_place(tmp_ref, block, store):
    cols = block.shape[0]
    strips = cols // WINDOW
    for t, part in enumerate(tiles(block)):
        tmp_ref[t] = part
    for b in range(WINDOW):
        store(b * strips, strips, strided(tmp_ref, b, strips, WINDOW))


def expand_kernel(x_ref, gain_ref, w1_ref, out_ref, n_ref, tmp_ref):
    rows, cols, _ = x_ref.shape

    @pl.when(pl.program_id(0) == 0)
    def _():
        gain = gain_ref[...]
        for i in range(rows):

            def store(at, count, part):
                n_ref[i * cols + at : i * cols + at + count, :] = part.astype(jnp.bfloat16)

            by_place(tmp_ref, normalize(x_ref[i].astype(jnp.float32), gain), store)

    w1 = w1_ref[...]
    for i in range(rows):
        hidden = jnp.dot(n_ref[i * cols : (i + 1) * cols, :], w1, preferred_element_type=jnp.float32)
        out_ref[i] = gelu(hidden.astype(jnp.bfloat16)).reshape(out_ref.shape[1:])


def expand_own(tokens, gain, w_expand):
    rows, cols, channels = tokens.shape
    width = w_expand.shape[1]
    features = min(EXPAND, width)
    strips = cols // WINDOW
    return pl.pallas_call(
        expand_kernel,
        grid=(width // features,),
        out_shape=jax.ShapeDtypeStruct((rows, WINDOW, strips, width), jnp.bfloat16),
        in_specs=[
            pl.BlockSpec(tokens.shape, lambda f: (0, 0, 0)),
            pl.BlockSpec((1, channels), lambda f: (0, 0)),
            pl.BlockSpec((channels, features), lambda f: (0, f)),
        ],
        out_specs=pl.BlockSpec((rows, WINDOW, strips, features), lambda f: (0, 0, 0, f)),
        scratch_shapes=[
            pltpu.VMEM((rows * cols, channels), jnp.bfloat16),
            pltpu.VMEM((channels // LANES, cols, LANES), jnp.float32),
        ],
        compiler_params=pltpu.CompilerParams(dimension_semantics=("arbitrary",), vmem_limit_bytes=56 * MIB),
        cost_estimate=pl.CostEstimate(
            flops=2 * rows * cols * channels * width,
            bytes_accessed=2 * channels * width + 2 * rows * cols * (channels + width),
            transcendentals=rows * cols * width,
        ),
        name="expand_own",
    )(tokens, gain.reshape(1, channels), w_expand)


def conv_kernel(
    conv_steps, shape, x_ref, e_ref, ns0_ref, ns1_ref, ew0_ref, ew1_ref, gain_ref, w1_ref, dw_ref, w2_ref,
    block_gain_ref, wqkv_hbm, wout_hbm, out_ref, n_ref, tmp_ref, edge_ref, side_ref, acc_ref, wqkv_ref, wout_ref, sems
):
    step = pl.program_id(0)
    rows, cols, channels = x_ref.shape
    strips = cols // WINDOW
    features = w1_ref.shape[1]
    side_rows = ew0_ref.shape[0]
    side_count = side_rows + -side_rows % 16
    copies = [
        pltpu.make_async_copy(wqkv_hbm, wqkv_ref, sems.at[0]),
        pltpu.make_async_copy(wout_hbm, wout_ref, sems.at[1]),
    ]

    @pl.when(step == 0)
    def _():
        for copy in copies:
            copy.start()
        gain = gain_ref[...]

        def sorted_pair(first_ref, second_ref, axis):
            first, second = first_ref[...].astype(jnp.float32), second_ref[...].astype(jnp.float32)
            even = lax.rem(lax.axis_index(axis), 2) == 0
            return jnp.where(even, second, first), jnp.where(even, first, second)

        for k, block in enumerate(sorted_pair(ns0_ref, ns1_ref, "ns")):

            def store(at, count, part):
                n_ref[k * cols + at : k * cols + at + count, :] = part.astype(jnp.bfloat16)

            by_place(tmp_ref, normalize(block, gain), store)
        pad = jnp.zeros((side_count - side_rows, channels), jnp.float32)
        for k, block in enumerate(sorted_pair(ew0_ref, ew1_ref, "ew")):
            start = 2 * cols + k * side_count
            n_ref[start : start + side_count, :] = normalize(
                jnp.concatenate([block, pad], axis=0), gain
            ).astype(jnp.bfloat16)
        for i in range(rows):

            def keep(at, count, part):
                for t, piece in enumerate(tiles(part)):
                    acc_ref[t, i * cols + at : i * cols + at + count, :] = piece

            by_place(tmp_ref, x_ref[i].astype(jnp.float32), keep)

    @pl.when(step < conv_steps)
    def _():
        w2 = w2_ref[...]
        taps = [[dw_ref[3 * a + b : 3 * a + b + 1, :].astype(jnp.bfloat16) for b in range(3)] for a in range(3)]
        halo = gelu(
            jnp.dot(n_ref[...], w1_ref[...], preferred_element_type=jnp.float32).astype(jnp.bfloat16)
        )
        for k in range(2):
            edge_ref[k] = halo[k * cols : (k + 1) * cols].reshape(WINDOW, strips, features)
        sides = halo[2 * cols :].astype(jnp.float32)
        place_in_strip = lax.broadcasted_iota(jnp.int32, (strips, features), 0)

        def own(i, b):
            if i == 0:
                return edge_ref[0, b]
            if i == rows + 1:
                return edge_ref[1, b]
            return e_ref[i - 1, b]

        for i in range(rows + 2):
            last = pltpu.roll(own(i, WINDOW - 1).astype(jnp.float32), 1, axis=0)
            first = pltpu.roll(own(i, 0).astype(jnp.float32), strips - 1, axis=0)
            low = jnp.where(place_in_strip == 0, sides[i : i + 1], last)
            high = jnp.where(place_in_strip == strips - 1, sides[side_count + i : side_count + i + 1], first)
            side_ref[i, 0] = low.astype(jnp.bfloat16)
            side_ref[i, 1] = high.astype(jnp.bfloat16)

        def at(i, b):
            if b < 0:
                return side_ref[i, 0]
            if b >= WINDOW:
                return side_ref[i, 1]
            return own(i, b)

        for i in range(rows):
            pieces = []
            for b in range(WINDOW):
                sums = []
                for da in range(3):
                    t = [at(i + da, b + db - 1) * taps[da][db] for db in range(3)]
                    sums.append(t[0] + t[1] + t[2])
                pieces.append(gelu(sums[0] + sums[1] + sums[2]))
            active = jnp.concatenate(pieces, axis=0)
            for t, part in enumerate(tiles(jnp.dot(active, w2, preferred_element_type=jnp.float32))):
                acc_ref[t, i * cols : (i + 1) * cols, :] += part

    @pl.when(step == conv_steps)
    def _():
        for copy in copies:
            copy.wait()

    @pl.when(step >= conv_steps)
    def _():
        all_places, across = shape
        _, places, shares, parts, side, _ = out_ref.shape
        size = rows * WINDOW
        first = (step - conv_steps) * places
        x = jnp.concatenate(
            [
                strided(acc_ref, share * across + part * all_places + first + j, size, strips)
                for j in range(places)
                for share in range(shares)
                for part in range(parts)
            ],
            axis=0,
        ).astype(jnp.bfloat16)
        result = attend_windows(x.astype(jnp.float32), block_gain_ref[...], wqkv_ref, wout_ref)
        result = result.astype(jnp.bfloat16).reshape(places, shares, parts, size // side, side, channels)
        for j in range(places):
            for share in range(shares):
                for part in range(parts):
                    out_ref[:, j, share, part] = result[j, share, part]


def conv_and_windows(tokens, expanded, swaps, gain, w_expand, dw_kernel, w_project, block_gain, w_qkv, w_out, shape):
    rows, cols, channels = tokens.shape
    places, shares, parts = shape
    width = w_expand.shape[1]
    features = min(FEATURES, width)
    strips = cols // WINDOW
    conv_steps = width // features
    block_places = max(1, min(places, GROUP // (shares * parts)))
    side_rows = swaps[2].shape[0]
    side_count = side_rows + -side_rows % 16
    whole = lambda *shape: pl.BlockSpec(shape, lambda step: (0,) * len(shape))
    block_of = lambda step: jnp.minimum(step, conv_steps - 1)
    tokens_of = rows * cols
    return pl.pallas_call(
        functools.partial(conv_kernel, conv_steps, (places, strips // shares)),
        grid=(conv_steps + places // block_places,),
        out_shape=jax.ShapeDtypeStruct((rows, places, shares, parts, WINDOW, channels), jnp.bfloat16),
        in_specs=[
            whole(*tokens.shape),
            pl.BlockSpec((rows, WINDOW, strips, features), lambda step: (0, 0, 0, block_of(step))),
            *[whole(*swap.shape) for swap in swaps],
            whole(1, channels),
            pl.BlockSpec((channels, features), lambda step: (0, block_of(step))),
            pl.BlockSpec((9, features), lambda step: (0, block_of(step))),
            pl.BlockSpec((features, channels), lambda step: (block_of(step), 0)),
            whole(1, channels),
            pl.BlockSpec(memory_space=pl.ANY),
            pl.BlockSpec(memory_space=pl.ANY),
        ],
        out_specs=pl.BlockSpec(
            (rows, block_places, shares, parts, WINDOW, channels),
            lambda step: (0, jnp.maximum(step - conv_steps, 0), 0, 0, 0, 0),
        ),
        scratch_shapes=[
            pltpu.VMEM((2 * cols + 2 * side_count, channels), jnp.bfloat16),
            pltpu.VMEM((channels // LANES, cols, LANES), jnp.float32),
            pltpu.VMEM((2, WINDOW, strips, features), jnp.bfloat16),
            pltpu.VMEM((rows + 2, 2, strips, features), jnp.bfloat16),
            pltpu.VMEM((channels // LANES, tokens_of, LANES), jnp.float32),
            pltpu.VMEM(w_qkv.shape, jnp.bfloat16),
            pltpu.VMEM(w_out.shape, jnp.bfloat16),
            pltpu.SemaphoreType.DMA((2,)),
        ],
        compiler_params=pltpu.CompilerParams(dimension_semantics=("arbitrary",), vmem_limit_bytes=56 * MIB),
        cost_estimate=pl.CostEstimate(
            flops=2 * tokens_of * channels * (width + 8 * channels),
            bytes_accessed=4 * channels * width + 2 * tokens_of * (2 * channels + width),
            transcendentals=tokens_of * width,
        ),
        name="conv_and_windows",
    )(
        tokens,
        expanded,
        *swaps,
        gain.reshape(1, channels),
        w_expand,
        dw_kernel.reshape(9, width),
        w_project,
        block_gain.reshape(1, channels),
        w_qkv,
        w_out,
    )


def attend_windows(x, gain, wqkv_ref, wout_ref):
    tokens, channels = x.shape
    head_dim = channels // HEADS
    group = LANES // head_dim
    size = WINDOW * WINDOW
    two = 2 * head_dim
    pairs, groups = tokens // (2 * size), channels // LANES
    units = [(p, g) for p in range(pairs) for g in range(groups)]
    scale = math.log2(math.e) / math.sqrt(head_dim)
    normed = normalize(x, gain).astype(jnp.bfloat16)

    def project(first):
        return jnp.dot(normed, wqkv_ref[:, first : first + channels], preferred_element_type=jnp.float32)

    queries = (project(0) * scale).astype(jnp.bfloat16)
    keys = project(channels).astype(jnp.bfloat16)
    values = lax.dot_general(
        wqkv_ref[:, 2 * channels :].T, normed, NT, preferred_element_type=jnp.float32
    ).astype(jnp.bfloat16)
    lane = lax.broadcasted_iota(jnp.int32, (1, LANES), 1)
    head_lanes = [(lane // head_dim == h).astype(jnp.float32).astype(jnp.bfloat16) for h in range(group)]
    halves = [(lane // size == h).astype(jnp.float32).astype(jnp.bfloat16) for h in range(2)]
    pick = (
        (
            lax.broadcasted_iota(jnp.int32, (size, 2 * size), 0)
            == lax.broadcasted_iota(jnp.int32, (size, 2 * size), 1) % size
        )
        .astype(jnp.float32)
        .astype(jnp.bfloat16)
    )
    scores = {}
    for p, g in units:
        for odd in range(2):
            at = (2 * p + odd) * size
            q = queries[at : at + size, g * LANES : (g + 1) * LANES]
            k = keys[at : at + size, g * LANES : (g + 1) * LANES]
            q_heads = jnp.concatenate([q * m for m in head_lanes], axis=0)
            scores[p, g, odd] = lax.dot_general(k, q_heads, NT, preferred_element_type=jnp.float32)
    weights = {}
    for unit, s in scores.items():
        raised = jnp.exp2(s - jnp.max(s, axis=0, keepdims=True))
        weights[unit] = (raised * (1.0 / jnp.sum(raised, axis=0, keepdims=True))).astype(jnp.bfloat16)
    mixed = {}
    for p, g in units:
        both = jnp.concatenate([weights[p, g, 0], weights[p, g, 1]], axis=0)
        for t in range(group // 2):
            at = g * LANES + t * two
            v = values[at : at + two, p * 2 * size : (p + 1) * 2 * size]
            v_halves = jnp.concatenate([v * m for m in halves], axis=0)
            mixed[p, g, t] = jnp.dot(
                v_halves, both[:, t * 2 * size : (t + 1) * 2 * size], preferred_element_type=jnp.float32
            ).astype(jnp.bfloat16)
    parts = {}
    for p, g in units:
        own = [
            mixed[p, g, t][odd * two + h * head_dim : odd * two + (h + 1) * head_dim] * halves[h]
            for odd in range(2)
            for t in range(group // 2)
            for h in range(2)
        ]
        parts[p, g] = lax.dot_general(
            pick, jnp.concatenate(own, axis=0), NT, preferred_element_type=jnp.float32
        ).astype(jnp.bfloat16)
    blended = [
        jnp.concatenate([parts[p, g][:, odd * LANES : (odd + 1) * LANES] for g in range(groups)], axis=1)
        for p in range(pairs)
        for odd in range(2)
    ]
    return x + jnp.dot(jnp.concatenate(blended, axis=0), wout_ref[...], preferred_element_type=jnp.float32)


def grid_kernel(x_ref, gain_ref, wqkv_ref, wout_ref, out_ref, floats_ref):
    step = pl.program_id(0)
    tokens, channels = x_ref.shape
    size = WINDOW * WINDOW
    windows = tokens // size
    block = windows // pl.num_programs(0)

    @pl.when(step == 0)
    def _():
        for t, part in enumerate(tiles(x_ref[...])):
            floats_ref[t] = part.astype(jnp.float32)

    first = step * block
    x = jnp.concatenate([strided(floats_ref, first + w, size, windows) for w in range(block)], axis=0)
    result = attend_windows(x, gain_ref[...], wqkv_ref, wout_ref)
    for t, part in enumerate(tiles(result)):
        for w in range(block):
            floats_ref[t, pl.ds(first + w, size, stride=windows), :] = part[w * size : (w + 1) * size]

    @pl.when(step == pl.num_programs(0) - 1)
    def _():
        for t in range(floats_ref.shape[0]):
            out_ref[:, t * LANES : (t + 1) * LANES] = floats_ref[t].astype(jnp.bfloat16)


def grid_attention(x, gain, w_qkv, w_out):
    tokens, channels = x.shape
    windows = tokens // (WINDOW * WINDOW)
    whole = lambda *shape: pl.BlockSpec(shape, lambda step: (0,) * len(shape))
    return pl.pallas_call(
        grid_kernel,
        grid=(windows // min(GROUP, windows),),
        out_shape=jax.ShapeDtypeStruct((tokens, channels), jnp.bfloat16),
        in_specs=[whole(tokens, channels), whole(1, channels), whole(*w_qkv.shape), whole(*w_out.shape)],
        out_specs=whole(tokens, channels),
        scratch_shapes=[pltpu.VMEM((channels // LANES, tokens, LANES), jnp.float32)],
        compiler_params=pltpu.CompilerParams(dimension_semantics=("arbitrary",), vmem_limit_bytes=24 * MIB),
        cost_estimate=pl.CostEstimate(
            flops=16 * tokens * channels * channels,
            bytes_accessed=8 * channels * channels + 4 * tokens * channels,
            transcendentals=HEADS * tokens * WINDOW * WINDOW,
        ),
        name="grid_attention",
    )(x, gain.reshape(1, channels), w_qkv, w_out)


def swap(low_edge, high_edge, axis, first):
    pairs = [(a, a + 1) for a in range(first, lax.axis_size(axis) - 1, 2)]
    lower = lax.rem(lax.axis_index(axis), 2) == first
    return lax.ppermute(
        jnp.where(lower, high_edge, low_edge), axis, pairs + [(target, source) for source, target in pairs]
    )


def halo(tokens):
    rows, cols, _ = tokens.shape
    ns0, ns1 = [swap(tokens[0], tokens[rows - 1], "ns", first) for first in range(2)]
    even = lax.rem(lax.axis_index("ns"), 2) == 0

    def column(c):
        north, south = jnp.where(even, ns1[c], ns0[c]), jnp.where(even, ns0[c], ns1[c])
        return jnp.concatenate([north[None], tokens[:, c], south[None]])

    ew0, ew1 = [swap(column(0), column(cols - 1), "ew", first) for first in range(2)]
    return ns0, ns1, ew0, ew1


def exchange(x):
    bands, strips = lax.axis_size("ns"), lax.axis_size("ew")
    if bands == WINDOW:
        return lax.all_to_all(x, ("ns", "ew"), 0, 0, tiled=True)
    inner = bands // WINDOW
    groups = [[a * inner + p for a in range(WINDOW)] for p in range(inner)]
    shape = x.shape
    x = x.reshape(WINDOW, strips, *shape[1:])
    x = lax.all_to_all(x, "ns", 0, 0, axis_index_groups=groups, tiled=True)
    x = lax.all_to_all(x, "ew", 1, 1, tiled=True)
    return x.reshape(shape)


def on_device(
    tokens,
    conv_gain,
    w_expand,
    dw_kernel,
    w_project,
    block_gain,
    block_qkv,
    block_out,
    grid_gain,
    grid_qkv,
    grid_out,
):
    rows, cols, channels = tokens.shape
    shares = WINDOW // lax.axis_size("ew")
    group = WINDOW * lax.axis_size("ew")
    across = cols // shares // WINDOW
    places = group // rows
    parts = across // places
    expanded = expand_own(tokens, conv_gain, w_expand)
    sent = conv_and_windows(
        tokens,
        expanded,
        halo(tokens),
        conv_gain,
        w_expand,
        dw_kernel,
        w_project,
        block_gain,
        block_qkv,
        block_out,
        (places, shares, parts),
    )
    x = exchange(sent.reshape(group, -1, channels))
    y = grid_attention(x.reshape(-1, channels), grid_gain, grid_qkv, grid_out)
    returned = exchange(y.reshape(group, -1, channels)).reshape(rows, places, shares, parts, WINDOW, channels)
    return jnp.transpose(returned, (0, 2, 3, 1, 4, 5)).reshape(rows, cols, channels)


def solution(mesh):
    in_specs = (P("ns", "ew", None), P(), P(), P(), P(), P(), P(), P(), P(), P(), P())
    out_specs = P("ns", "ew", None)
    return jax.shard_map(
        on_device, mesh=mesh, in_specs=in_specs, out_specs=out_specs, check_vma=False
    )
```

```python
import functools
import math

import jax
import jax.numpy as jnp
from jax import lax
from jax.experimental import pallas as pl
from jax.experimental.pallas import tpu as pltpu
from jax.sharding import PartitionSpec as P

HEADS = 16
WINDOW = 8
FEATURES = 1024
LANES = 128
GROUP = 8
MIB = 1024 * 1024

NT = (((1,), (1,)), ((), ()))


def normalize(floats, scale_gain):
    center = floats - jnp.mean(floats, axis=-1, keepdims=True)
    spread = jnp.mean(center * center, axis=-1, keepdims=True)
    return center * lax.rsqrt(spread + 1e-05) * scale_gain


def gelu(v):
    inner = v * (math.sqrt(2 / math.pi) + (math.sqrt(2 / math.pi) * 0.044715) * (v * v))
    half = 0.5 * v
    return half + half * jnp.tanh(inner)


def tiles(value):
    return [value[:, t : t + LANES] for t in range(0, value.shape[1], LANES)]


def strided(ref, start, size, stride):
    return jnp.concatenate([ref[t, pl.ds(start, size, stride=stride), :] for t in range(ref.shape[0])], axis=1)


def by_place(tmp_ref, block, store):
    cols = block.shape[0]
    strips = cols // WINDOW
    for t, part in enumerate(tiles(block)):
        tmp_ref[t] = part
    for b in range(WINDOW):
        store(b * strips, strips, strided(tmp_ref, b, strips, WINDOW))


def conv_kernel(
    conv_steps, shape, x_hbm, ns0_ref, ns1_ref, ew0_ref, ew1_ref, gain_ref, w1_hbm, dw_ref, w2_hbm, block_gain_ref,
    wqkv_hbm, wout_hbm, out_ref, n_ref, tmp_ref, e_ref, acc_ref, x_ref, w1_ref, w2_ref, wqkv_ref, wout_ref, sems
):
    step = pl.program_id(0)
    rows, cols, channels = x_ref.shape
    strips = cols // WINDOW
    features = w1_ref.shape[2]
    side_rows = ew0_ref.shape[0]
    side_count = side_rows + -side_rows % 16
    copy_x = pltpu.make_async_copy(x_hbm, x_ref, sems.at[0])
    copies_late = [
        pltpu.make_async_copy(wqkv_hbm, wqkv_ref, sems.at[1]),
        pltpu.make_async_copy(wout_hbm, wout_ref, sems.at[2]),
    ]
    copies_w1 = [
        pltpu.make_async_copy(w1_hbm.at[:, f * features : (f + 1) * features], w1_ref.at[f], sems.at[3 + f])
        for f in range(conv_steps)
    ]
    copies_w2 = [
        pltpu.make_async_copy(w2_hbm.at[f * features : (f + 1) * features], w2_ref.at[f], sems.at[3 + conv_steps + f])
        for f in range(conv_steps)
    ]

    @pl.when(step == 0)
    def _():
        copy_x.start()
        for f in range(conv_steps):
            copies_w1[f].start()
            copies_w2[f].start()
        for copy in copies_late:
            copy.start()
        gain = gain_ref[...]

        def place(slot, block):
            def store(at, count, part):
                n_ref[slot * cols + at : slot * cols + at + count, :] = part.astype(jnp.bfloat16)

            by_place(tmp_ref, normalize(block, gain), store)

        def sorted_pair(first_ref, second_ref, axis):
            first, second = first_ref[...].astype(jnp.float32), second_ref[...].astype(jnp.float32)
            even = lax.rem(lax.axis_index(axis), 2) == 0
            return jnp.where(even, second, first), jnp.where(even, first, second)

        north, south = sorted_pair(ns0_ref, ns1_ref, "ns")
        place(0, north)
        place(rows + 1, south)
        pad = jnp.zeros((side_count - side_rows, channels), jnp.float32)
        for k, block in enumerate(sorted_pair(ew0_ref, ew1_ref, "ew")):
            start = (rows + 2) * cols + k * side_count
            n_ref[start : start + side_count, :] = normalize(
                jnp.concatenate([block, pad], axis=0), gain
            ).astype(jnp.bfloat16)
        copy_x.wait()
        for i in range(rows):
            block = x_ref[i].astype(jnp.float32)
            place(i + 1, block)

            def keep(at, count, part):
                for t, piece in enumerate(tiles(part)):
                    acc_ref[t, i * cols + at : i * cols + at + count, :] = piece

            by_place(tmp_ref, block, keep)

    for f in range(conv_steps):

        @pl.when(step == f)
        def _():
            copies_w1[f].wait()
            copies_w2[f].wait()

    @pl.when(step < conv_steps)
    def _():
        w1 = w1_ref[step]
        w2 = w2_ref[step]
        taps = [[dw_ref[a, b : b + 1, :].astype(jnp.bfloat16) for b in range(3)] for a in range(3)]

        def hidden(first, count):
            return gelu(
                jnp.dot(n_ref[first : first + count, :], w1, preferred_element_type=jnp.float32).astype(jnp.bfloat16)
            )

        sides = hidden((rows + 2) * cols, 2 * side_count).astype(jnp.float32)
        place_in_strip = lax.broadcasted_iota(jnp.int32, (strips, features), 0)
        for i in range(rows + 2):
            own = hidden(i * cols, cols)
            e_ref[i, 1 : WINDOW + 1] = own.reshape(WINDOW, strips, features)
            last = pltpu.roll(own[(WINDOW - 1) * strips :].astype(jnp.float32), 1, axis=0)
            first = pltpu.roll(own[:strips].astype(jnp.float32), strips - 1, axis=0)
            low = jnp.where(place_in_strip == 0, sides[i : i + 1], last)
            high = jnp.where(place_in_strip == strips - 1, sides[side_count + i : side_count + i + 1], first)
            e_ref[i, 0] = low.astype(jnp.bfloat16)
            e_ref[i, WINDOW + 1] = high.astype(jnp.bfloat16)
        for i in range(rows):
            pieces = []
            for b in range(WINDOW):
                sums = []
                for da in range(3):
                    t = [e_ref[i + da, b + db] * taps[da][db] for db in range(3)]
                    sums.append(t[0] + t[1] + t[2])
                pieces.append(gelu(sums[0] + sums[1] + sums[2]))
            active = jnp.concatenate(pieces, axis=0)
            for t, part in enumerate(tiles(jnp.dot(active, w2, preferred_element_type=jnp.float32))):
                acc_ref[t, i * cols : (i + 1) * cols, :] += part

    @pl.when(step == conv_steps)
    def _():
        for copy in copies_late:
            copy.wait()

    @pl.when(step >= conv_steps)
    def _():
        all_places, across = shape
        _, places, shares, parts, side, _ = out_ref.shape
        size = rows * WINDOW
        first = (step - conv_steps) * places
        x = jnp.concatenate(
            [
                strided(acc_ref, share * across + part * all_places + first + j, size, strips)
                for j in range(places)
                for share in range(shares)
                for part in range(parts)
            ],
            axis=0,
        ).astype(jnp.bfloat16)
        result = attend_windows(x.astype(jnp.float32), block_gain_ref[...], wqkv_ref, wout_ref)
        result = result.astype(jnp.bfloat16).reshape(places, shares, parts, size // side, side, channels)
        for j in range(places):
            for share in range(shares):
                for part in range(parts):
                    out_ref[:, j, share, part] = result[j, share, part]


def conv_and_windows(tokens, swaps, gain, w_expand, dw_kernel, w_project, block_gain, w_qkv, w_out, shape):
    rows, cols, channels = tokens.shape
    places, shares, parts = shape
    width = w_expand.shape[1]
    features = min(FEATURES, width)
    strips = cols // WINDOW
    conv_steps = width // features
    block_places = max(1, min(places, GROUP // (shares * parts)))
    side_rows = swaps[2].shape[0]
    side_count = side_rows + -side_rows % 16
    whole = lambda *shape: pl.BlockSpec(shape, lambda step: (0,) * len(shape))
    anywhere = pl.BlockSpec(memory_space=pl.ANY)
    tokens_of = rows * cols
    return pl.pallas_call(
        functools.partial(conv_kernel, conv_steps, (places, strips // shares)),
        grid=(conv_steps + places // block_places,),
        out_shape=jax.ShapeDtypeStruct((rows, places, shares, parts, WINDOW, channels), jnp.bfloat16),
        in_specs=[
            anywhere,
            *[whole(*swap.shape) for swap in swaps],
            whole(1, channels),
            anywhere,
            pl.BlockSpec((3, 3, features), lambda step: (0, 0, jnp.minimum(step, conv_steps - 1))),
            anywhere,
            whole(1, channels),
            anywhere,
            anywhere,
        ],
        out_specs=pl.BlockSpec(
            (rows, block_places, shares, parts, WINDOW, channels),
            lambda step: (0, jnp.maximum(step - conv_steps, 0), 0, 0, 0, 0),
        ),
        scratch_shapes=[
            pltpu.VMEM(((rows + 2) * cols + 2 * side_count, channels), jnp.bfloat16),
            pltpu.VMEM((channels // LANES, cols, LANES), jnp.float32),
            pltpu.VMEM((rows + 2, WINDOW + 2, strips, features), jnp.bfloat16),
            pltpu.VMEM((channels // LANES, tokens_of, LANES), jnp.float32),
            pltpu.VMEM(tokens.shape, jnp.bfloat16),
            pltpu.VMEM((conv_steps, channels, features), jnp.bfloat16),
            pltpu.VMEM((conv_steps, features, channels), jnp.bfloat16),
            pltpu.VMEM(w_qkv.shape, jnp.bfloat16),
            pltpu.VMEM(w_out.shape, jnp.bfloat16),
            pltpu.SemaphoreType.DMA((3 + 2 * conv_steps,)),
        ],
        compiler_params=pltpu.CompilerParams(dimension_semantics=("arbitrary",), vmem_limit_bytes=56 * MIB),
        cost_estimate=pl.CostEstimate(
            flops=4 * tokens_of * channels * (width + 4 * channels),
            bytes_accessed=4 * channels * (width + 2 * channels) + 4 * tokens_of * channels,
            transcendentals=2 * tokens_of * width,
        ),
        name="conv_and_windows",
    )(
        tokens,
        *swaps,
        gain.reshape(1, channels),
        w_expand,
        dw_kernel,
        w_project,
        block_gain.reshape(1, channels),
        w_qkv,
        w_out,
    )


def attend_windows(x, gain, wqkv_ref, wout_ref):
    tokens, channels = x.shape
    head_dim = channels // HEADS
    group = LANES // head_dim
    size = WINDOW * WINDOW
    two = 2 * head_dim
    pairs, groups = tokens // (2 * size), channels // LANES
    units = [(p, g) for p in range(pairs) for g in range(groups)]
    scale = math.log2(math.e) / math.sqrt(head_dim)
    normed = normalize(x, gain).astype(jnp.bfloat16)

    def project(first):
        return jnp.dot(normed, wqkv_ref[:, first : first + channels], preferred_element_type=jnp.float32)

    queries = (project(0) * scale).astype(jnp.bfloat16)
    keys = project(channels).astype(jnp.bfloat16)
    values = lax.dot_general(
        wqkv_ref[:, 2 * channels :].T, normed, NT, preferred_element_type=jnp.float32
    ).astype(jnp.bfloat16)
    lane = lax.broadcasted_iota(jnp.int32, (1, LANES), 1)
    head_lanes = [(lane // head_dim == h).astype(jnp.float32).astype(jnp.bfloat16) for h in range(group)]
    halves = [(lane // size == h).astype(jnp.float32).astype(jnp.bfloat16) for h in range(2)]
    pick = (
        (
            lax.broadcasted_iota(jnp.int32, (size, 2 * size), 0)
            == lax.broadcasted_iota(jnp.int32, (size, 2 * size), 1) % size
        )
        .astype(jnp.float32)
        .astype(jnp.bfloat16)
    )
    scores = {}
    for p, g in units:
        for odd in range(2):
            at = (2 * p + odd) * size
            q = queries[at : at + size, g * LANES : (g + 1) * LANES]
            k = keys[at : at + size, g * LANES : (g + 1) * LANES]
            q_heads = jnp.concatenate([q * m for m in head_lanes], axis=0)
            scores[p, g, odd] = lax.dot_general(k, q_heads, NT, preferred_element_type=jnp.float32)
    weights = {}
    for unit, s in scores.items():
        raised = jnp.exp2(s - jnp.max(s, axis=0, keepdims=True))
        weights[unit] = (raised * (1.0 / jnp.sum(raised, axis=0, keepdims=True))).astype(jnp.bfloat16)
    mixed = {}
    for p, g in units:
        both = jnp.concatenate([weights[p, g, 0], weights[p, g, 1]], axis=0)
        for t in range(group // 2):
            at = g * LANES + t * two
            v = values[at : at + two, p * 2 * size : (p + 1) * 2 * size]
            v_halves = jnp.concatenate([v * m for m in halves], axis=0)
            mixed[p, g, t] = jnp.dot(
                v_halves, both[:, t * 2 * size : (t + 1) * 2 * size], preferred_element_type=jnp.float32
            ).astype(jnp.bfloat16)
    parts = {}
    for p, g in units:
        own = [
            mixed[p, g, t][odd * two + h * head_dim : odd * two + (h + 1) * head_dim] * halves[h]
            for odd in range(2)
            for t in range(group // 2)
            for h in range(2)
        ]
        parts[p, g] = lax.dot_general(
            pick, jnp.concatenate(own, axis=0), NT, preferred_element_type=jnp.float32
        ).astype(jnp.bfloat16)
    blended = [
        jnp.concatenate([parts[p, g][:, odd * LANES : (odd + 1) * LANES] for g in range(groups)], axis=1)
        for p in range(pairs)
        for odd in range(2)
    ]
    return x + jnp.dot(jnp.concatenate(blended, axis=0), wout_ref[...], preferred_element_type=jnp.float32)


def grid_kernel(x_ref, gain_ref, wqkv_ref, wout_ref, out_ref, floats_ref):
    step = pl.program_id(0)
    tokens, channels = x_ref.shape
    size = WINDOW * WINDOW
    windows = tokens // size
    block = windows // pl.num_programs(0)

    @pl.when(step == 0)
    def _():
        for t, part in enumerate(tiles(x_ref[...])):
            floats_ref[t] = part.astype(jnp.float32)

    first = step * block
    x = jnp.concatenate([strided(floats_ref, first + w, size, windows) for w in range(block)], axis=0)
    result = attend_windows(x, gain_ref[...], wqkv_ref, wout_ref)
    for t, part in enumerate(tiles(result)):
        for w in range(block):
            floats_ref[t, pl.ds(first + w, size, stride=windows), :] = part[w * size : (w + 1) * size]

    @pl.when(step == pl.num_programs(0) - 1)
    def _():
        for t in range(floats_ref.shape[0]):
            out_ref[:, t * LANES : (t + 1) * LANES] = floats_ref[t].astype(jnp.bfloat16)


def grid_attention(x, gain, w_qkv, w_out):
    tokens, channels = x.shape
    windows = tokens // (WINDOW * WINDOW)
    whole = lambda *shape: pl.BlockSpec(shape, lambda step: (0,) * len(shape))
    return pl.pallas_call(
        grid_kernel,
        grid=(windows // min(GROUP, windows),),
        out_shape=jax.ShapeDtypeStruct((tokens, channels), jnp.bfloat16),
        in_specs=[whole(tokens, channels), whole(1, channels), whole(*w_qkv.shape), whole(*w_out.shape)],
        out_specs=whole(tokens, channels),
        scratch_shapes=[pltpu.VMEM((channels // LANES, tokens, LANES), jnp.float32)],
        compiler_params=pltpu.CompilerParams(dimension_semantics=("arbitrary",), vmem_limit_bytes=24 * MIB),
        cost_estimate=pl.CostEstimate(
            flops=16 * tokens * channels * channels,
            bytes_accessed=8 * channels * channels + 4 * tokens * channels,
            transcendentals=HEADS * tokens * WINDOW * WINDOW,
        ),
        name="grid_attention",
    )(x, gain.reshape(1, channels), w_qkv, w_out)


def swap(low_edge, high_edge, axis, first):
    pairs = [(a, a + 1) for a in range(first, lax.axis_size(axis) - 1, 2)]
    lower = lax.rem(lax.axis_index(axis), 2) == first
    return lax.ppermute(
        jnp.where(lower, high_edge, low_edge), axis, pairs + [(target, source) for source, target in pairs]
    )


def halo(tokens):
    rows, cols, _ = tokens.shape
    ns0, ns1 = [swap(tokens[0], tokens[rows - 1], "ns", first) for first in range(2)]
    even = lax.rem(lax.axis_index("ns"), 2) == 0

    def column(c):
        north, south = jnp.where(even, ns1[c], ns0[c]), jnp.where(even, ns0[c], ns1[c])
        return jnp.concatenate([north[None], tokens[:, c], south[None]])

    ew0, ew1 = [swap(column(0), column(cols - 1), "ew", first) for first in range(2)]
    return ns0, ns1, ew0, ew1


def exchange(x):
    bands, strips = lax.axis_size("ns"), lax.axis_size("ew")
    if bands == WINDOW:
        return lax.all_to_all(x, ("ns", "ew"), 0, 0, tiled=True)
    inner = bands // WINDOW
    groups = [[a * inner + p for a in range(WINDOW)] for p in range(inner)]
    shape = x.shape
    x = x.reshape(WINDOW, strips, *shape[1:])
    x = lax.all_to_all(x, "ns", 0, 0, axis_index_groups=groups, tiled=True)
    x = lax.all_to_all(x, "ew", 1, 1, tiled=True)
    return x.reshape(shape)


def on_device(
    tokens,
    conv_gain,
    w_expand,
    dw_kernel,
    w_project,
    block_gain,
    block_qkv,
    block_out,
    grid_gain,
    grid_qkv,
    grid_out,
):
    rows, cols, channels = tokens.shape
    shares = WINDOW // lax.axis_size("ew")
    group = WINDOW * lax.axis_size("ew")
    across = cols // shares // WINDOW
    places = group // rows
    parts = across // places
    sent = conv_and_windows(
        tokens,
        halo(tokens),
        conv_gain,
        w_expand,
        dw_kernel,
        w_project,
        block_gain,
        block_qkv,
        block_out,
        (places, shares, parts),
    )
    x = exchange(sent.reshape(group, -1, channels))
    y = grid_attention(x.reshape(-1, channels), grid_gain, grid_qkv, grid_out)
    returned = exchange(y.reshape(group, -1, channels)).reshape(rows, places, shares, parts, WINDOW, channels)
    return jnp.transpose(returned, (0, 2, 3, 1, 4, 5)).reshape(rows, cols, channels)


def solution(mesh):
    in_specs = (P("ns", "ew", None), P(), P(), P(), P(), P(), P(), P(), P(), P(), P())
    out_specs = P("ns", "ew", None)
    return jax.shard_map(
        on_device, mesh=mesh, in_specs=in_specs, out_specs=out_specs, check_vma=False
    )
```

```python
import functools
import math

import jax
import jax.numpy as jnp
from jax import lax
from jax.experimental import pallas as pl
from jax.experimental.pallas import tpu as pltpu
from jax.sharding import PartitionSpec as P

HEADS = 16
WINDOW = 8
FEATURES = 1024
LANES = 128
GROUP = 8
MIB = 1024 * 1024
NORM_LIMIT = 8
NORM_COST = 10_000_000_000
CONV_LIMIT = 32

NT = (((1,), (1,)), ((), ()))


def normalize(floats, scale_gain):
    center = floats - jnp.mean(floats, axis=-1, keepdims=True)
    spread = jnp.mean(center * center, axis=-1, keepdims=True)
    return center * lax.rsqrt(spread + 1e-05) * scale_gain


def gelu(v):
    inner = v * (math.sqrt(2 / math.pi) + (math.sqrt(2 / math.pi) * 0.044715) * (v * v))
    half = 0.5 * v
    return half + half * jnp.tanh(inner)


def tiles(value):
    return [value[:, t : t + LANES] for t in range(0, value.shape[1], LANES)]


def strided(ref, start, size, stride):
    return jnp.concatenate([ref[t, pl.ds(start, size, stride=stride), :] for t in range(ref.shape[0])], axis=1)


def by_place(tmp_ref, block, store):
    cols = block.shape[0]
    strips = cols // WINDOW
    for t, part in enumerate(tiles(block)):
        tmp_ref[t] = part
    for b in range(WINDOW):
        store(b * strips, strips, strided(tmp_ref, b, strips, WINDOW))


def norm_kernel(x_ref, gain_ref, normed_ref, moved_ref, tmp_ref):
    rows, cols, _ = x_ref.shape
    gain = gain_ref[...]
    for i in range(rows):

        block = x_ref[i].astype(jnp.float32)
        for out_ref, value in ((normed_ref, normalize(block, gain)), (moved_ref, block)):

            def store(at, count, part):
                out_ref[i * cols + at : i * cols + at + count, :] = part.astype(jnp.bfloat16)

            by_place(tmp_ref, value, store)


def norm_own(tokens, gain):
    rows, cols, channels = tokens.shape
    return pl.pallas_call(
        norm_kernel,
        out_shape=[jax.ShapeDtypeStruct((rows * cols, channels), jnp.bfloat16)] * 2,
        scratch_shapes=[pltpu.VMEM((channels // LANES, cols, LANES), jnp.float32)],
        compiler_params=pltpu.CompilerParams(vmem_limit_bytes=NORM_LIMIT * MIB),
        cost_estimate=pl.CostEstimate(flops=NORM_COST, bytes_accessed=4 * rows * cols * channels, transcendentals=0),
        name="norm_own",
    )(tokens, gain.reshape(1, channels))


def conv_kernel(
    conv_steps, shape, x_ref, own_ref, ns0_ref, ns1_ref, ew0_ref, ew1_ref, gain_ref, w1_ref, dw_ref, w2_ref,
    block_gain_ref, wqkv_ref, wout_ref, out_ref, n_ref, tmp_ref, e_ref, acc_ref
):
    step = pl.program_id(0)
    tokens, channels = x_ref.shape
    rows = out_ref.shape[0]
    cols = tokens // rows
    strips = cols // WINDOW
    features = w1_ref.shape[1] // conv_steps
    side_rows = ew0_ref.shape[0]
    side_count = side_rows + -side_rows % 16

    @pl.when(step == 0)
    def _():
        gain = gain_ref[...]

        def sorted_pair(first_ref, second_ref, axis):
            first, second = first_ref[...].astype(jnp.float32), second_ref[...].astype(jnp.float32)
            even = lax.rem(lax.axis_index(axis), 2) == 0
            return jnp.where(even, second, first), jnp.where(even, first, second)

        for k, block in enumerate(sorted_pair(ns0_ref, ns1_ref, "ns")):

            def store(at, count, part):
                n_ref[k * cols + at : k * cols + at + count, :] = part.astype(jnp.bfloat16)

            by_place(tmp_ref, normalize(block, gain), store)
        pad = jnp.zeros((side_count - side_rows, channels), jnp.float32)
        for k, block in enumerate(sorted_pair(ew0_ref, ew1_ref, "ew")):
            start = 2 * cols + k * side_count
            n_ref[start : start + side_count, :] = normalize(
                jnp.concatenate([block, pad], axis=0), gain
            ).astype(jnp.bfloat16)
        for t in range(channels // LANES):
            acc_ref[t] = x_ref[:, t * LANES : (t + 1) * LANES].astype(jnp.float32)

    @pl.when(step < conv_steps)
    def _():
        block = pl.ds(pl.multiple_of(step * features, features), features)
        w1 = w1_ref[:, block]
        w2 = w2_ref[block, :]
        taps = [[dw_ref[a, b : b + 1, :].astype(jnp.bfloat16) for b in range(3)] for a in range(3)]

        def hidden(normed):
            return gelu(jnp.dot(normed, w1, preferred_element_type=jnp.float32).astype(jnp.bfloat16))

        sides = hidden(n_ref[2 * cols :, :]).astype(jnp.float32)
        place_in_strip = lax.broadcasted_iota(jnp.int32, (strips, features), 0)
        for i in range(rows + 2):
            if i in (0, rows + 1):
                edge = i // (rows + 1)
                own = hidden(n_ref[edge * cols : (edge + 1) * cols, :])
            else:
                own = hidden(own_ref[(i - 1) * cols : i * cols, :])
            e_ref[i, 1 : WINDOW + 1] = own.reshape(WINDOW, strips, features)
            last = pltpu.roll(own[(WINDOW - 1) * strips :].astype(jnp.float32), 1, axis=0)
            first = pltpu.roll(own[:strips].astype(jnp.float32), strips - 1, axis=0)
            low = jnp.where(place_in_strip == 0, sides[i : i + 1], last)
            high = jnp.where(place_in_strip == strips - 1, sides[side_count + i : side_count + i + 1], first)
            e_ref[i, 0] = low.astype(jnp.bfloat16)
            e_ref[i, WINDOW + 1] = high.astype(jnp.bfloat16)
        for i in range(rows):
            pieces = []
            for b in range(WINDOW):
                sums = []
                for da in range(3):
                    t = [e_ref[i + da, b + db] * taps[da][db] for db in range(3)]
                    sums.append(t[0] + t[1] + t[2])
                pieces.append(gelu(sums[0] + sums[1] + sums[2]))
            active = jnp.concatenate(pieces, axis=0)
            for t, part in enumerate(tiles(jnp.dot(active, w2, preferred_element_type=jnp.float32))):
                acc_ref[t, i * cols : (i + 1) * cols, :] += part

    @pl.when(step >= conv_steps)
    def _():
        all_places, across = shape
        _, places, shares, parts, side, _ = out_ref.shape
        size = rows * WINDOW
        first = (step - conv_steps) * places
        x = jnp.concatenate(
            [
                strided(acc_ref, share * across + part * all_places + first + j, size, strips)
                for j in range(places)
                for share in range(shares)
                for part in range(parts)
            ],
            axis=0,
        ).astype(jnp.bfloat16)
        result = attend_windows(x.astype(jnp.float32), block_gain_ref[...], wqkv_ref, wout_ref)
        result = result.astype(jnp.bfloat16).reshape(places, shares, parts, size // side, side, channels)
        for j in range(places):
            for share in range(shares):
                for part in range(parts):
                    out_ref[:, j, share, part] = result[j, share, part]


def conv_and_windows(moved, own, swaps, gain, w_expand, dw_kernel, w_project, block_gain, w_qkv, w_out, rows, shape):
    tokens, channels = moved.shape
    cols = tokens // rows
    places, shares, parts = shape
    width = w_expand.shape[1]
    features = min(FEATURES, width)
    strips = cols // WINDOW
    conv_steps = width // features
    block_places = max(1, min(places, GROUP // (shares * parts)))
    side_rows = swaps[2].shape[0]
    side_count = side_rows + -side_rows % 16
    vmem = pl.BlockSpec(memory_space=pltpu.VMEM)
    return pl.pallas_call(
        functools.partial(conv_kernel, conv_steps, (places, strips // shares)),
        grid=(conv_steps + places // block_places,),
        out_shape=jax.ShapeDtypeStruct((rows, places, shares, parts, WINDOW, channels), jnp.bfloat16),
        in_specs=[
            vmem,
            vmem,
            *[vmem for swap in swaps],
            vmem,
            vmem,
            pl.BlockSpec((3, 3, features), lambda step: (0, 0, jnp.minimum(step, conv_steps - 1))),
            vmem,
            vmem,
            vmem,
            vmem,
        ],
        out_specs=pl.BlockSpec(
            (rows, block_places, shares, parts, WINDOW, channels),
            lambda step: (0, jnp.maximum(step - conv_steps, 0), 0, 0, 0, 0),
        ),
        scratch_shapes=[
            pltpu.VMEM((2 * cols + 2 * side_count, channels), jnp.bfloat16),
            pltpu.VMEM((channels // LANES, cols, LANES), jnp.float32),
            pltpu.VMEM((rows + 2, WINDOW + 2, strips, features), jnp.bfloat16),
            pltpu.VMEM((channels // LANES, tokens, LANES), jnp.float32),
        ],
        compiler_params=pltpu.CompilerParams(dimension_semantics=("arbitrary",), vmem_limit_bytes=CONV_LIMIT * MIB),
        cost_estimate=pl.CostEstimate(
            flops=4 * tokens * channels * (width + 4 * channels),
            bytes_accessed=4 * channels * (width + 2 * channels) + 4 * tokens * channels,
            transcendentals=2 * tokens * width,
        ),
        name="conv_and_windows",
    )(
        moved,
        own,
        *swaps,
        gain.reshape(1, channels),
        w_expand,
        dw_kernel,
        w_project,
        block_gain.reshape(1, channels),
        w_qkv,
        w_out,
    )


def attend_windows(x, gain, wqkv_ref, wout_ref):
    tokens, channels = x.shape
    head_dim = channels // HEADS
    group = LANES // head_dim
    size = WINDOW * WINDOW
    two = 2 * head_dim
    pairs, groups = tokens // (2 * size), channels // LANES
    units = [(p, g) for p in range(pairs) for g in range(groups)]
    scale = math.log2(math.e) / math.sqrt(head_dim)
    normed = normalize(x, gain).astype(jnp.bfloat16)

    def project(first):
        return jnp.dot(normed, wqkv_ref[:, first : first + channels], preferred_element_type=jnp.float32)

    queries = (project(0) * scale).astype(jnp.bfloat16)
    keys = project(channels).astype(jnp.bfloat16)
    values = lax.dot_general(
        wqkv_ref[:, 2 * channels :].T, normed, NT, preferred_element_type=jnp.float32
    ).astype(jnp.bfloat16)
    lane = lax.broadcasted_iota(jnp.int32, (1, LANES), 1)
    head_lanes = [(lane // head_dim == h).astype(jnp.float32).astype(jnp.bfloat16) for h in range(group)]
    halves = [(lane // size == h).astype(jnp.float32).astype(jnp.bfloat16) for h in range(2)]
    pick = (
        (
            lax.broadcasted_iota(jnp.int32, (size, 2 * size), 0)
            == lax.broadcasted_iota(jnp.int32, (size, 2 * size), 1) % size
        )
        .astype(jnp.float32)
        .astype(jnp.bfloat16)
    )
    scores = {}
    for p, g in units:
        for odd in range(2):
            at = (2 * p + odd) * size
            q = queries[at : at + size, g * LANES : (g + 1) * LANES]
            k = keys[at : at + size, g * LANES : (g + 1) * LANES]
            q_heads = jnp.concatenate([q * m for m in head_lanes], axis=0)
            scores[p, g, odd] = lax.dot_general(k, q_heads, NT, preferred_element_type=jnp.float32)
    weights = {}
    for unit, s in scores.items():
        raised = jnp.exp2(s - jnp.max(s, axis=0, keepdims=True))
        weights[unit] = (raised * (1.0 / jnp.sum(raised, axis=0, keepdims=True))).astype(jnp.bfloat16)
    mixed = {}
    for p, g in units:
        both = jnp.concatenate([weights[p, g, 0], weights[p, g, 1]], axis=0)
        for t in range(group // 2):
            at = g * LANES + t * two
            v = values[at : at + two, p * 2 * size : (p + 1) * 2 * size]
            v_halves = jnp.concatenate([v * m for m in halves], axis=0)
            mixed[p, g, t] = jnp.dot(
                v_halves, both[:, t * 2 * size : (t + 1) * 2 * size], preferred_element_type=jnp.float32
            ).astype(jnp.bfloat16)
    parts = {}
    for p, g in units:
        own = [
            mixed[p, g, t][odd * two + h * head_dim : odd * two + (h + 1) * head_dim] * halves[h]
            for odd in range(2)
            for t in range(group // 2)
            for h in range(2)
        ]
        parts[p, g] = lax.dot_general(
            pick, jnp.concatenate(own, axis=0), NT, preferred_element_type=jnp.float32
        ).astype(jnp.bfloat16)
    blended = [
        jnp.concatenate([parts[p, g][:, odd * LANES : (odd + 1) * LANES] for g in range(groups)], axis=1)
        for p in range(pairs)
        for odd in range(2)
    ]
    return x + jnp.dot(jnp.concatenate(blended, axis=0), wout_ref[...], preferred_element_type=jnp.float32)


def grid_kernel(x_ref, gain_ref, wqkv_ref, wout_ref, out_ref, floats_ref):
    step = pl.program_id(0)
    tokens, channels = x_ref.shape
    size = WINDOW * WINDOW
    windows = tokens // size
    block = windows // pl.num_programs(0)

    @pl.when(step == 0)
    def _():
        for t, part in enumerate(tiles(x_ref[...])):
            floats_ref[t] = part.astype(jnp.float32)

    first = step * block
    x = jnp.concatenate([strided(floats_ref, first + w, size, windows) for w in range(block)], axis=0)
    result = attend_windows(x, gain_ref[...], wqkv_ref, wout_ref)
    for t, part in enumerate(tiles(result)):
        for w in range(block):
            floats_ref[t, pl.ds(first + w, size, stride=windows), :] = part[w * size : (w + 1) * size]

    @pl.when(step == pl.num_programs(0) - 1)
    def _():
        for t in range(floats_ref.shape[0]):
            out_ref[:, t * LANES : (t + 1) * LANES] = floats_ref[t].astype(jnp.bfloat16)


def grid_attention(x, gain, w_qkv, w_out):
    tokens, channels = x.shape
    windows = tokens // (WINDOW * WINDOW)
    whole = lambda *shape: pl.BlockSpec(shape, lambda step: (0,) * len(shape))
    return pl.pallas_call(
        grid_kernel,
        grid=(windows // min(GROUP, windows),),
        out_shape=jax.ShapeDtypeStruct((tokens, channels), jnp.bfloat16),
        in_specs=[whole(tokens, channels), whole(1, channels), whole(*w_qkv.shape), whole(*w_out.shape)],
        out_specs=whole(tokens, channels),
        scratch_shapes=[pltpu.VMEM((channels // LANES, tokens, LANES), jnp.float32)],
        compiler_params=pltpu.CompilerParams(dimension_semantics=("arbitrary",), vmem_limit_bytes=24 * MIB),
        cost_estimate=pl.CostEstimate(
            flops=16 * tokens * channels * channels,
            bytes_accessed=8 * channels * channels + 4 * tokens * channels,
            transcendentals=HEADS * tokens * WINDOW * WINDOW,
        ),
        name="grid_attention",
    )(x, gain.reshape(1, channels), w_qkv, w_out)


def swap(low_edge, high_edge, axis, first):
    pairs = [(a, a + 1) for a in range(first, lax.axis_size(axis) - 1, 2)]
    lower = lax.rem(lax.axis_index(axis), 2) == first
    return lax.ppermute(
        jnp.where(lower, high_edge, low_edge), axis, pairs + [(target, source) for source, target in pairs]
    )


def swap_columns(tokens, ns0, ns1):
    cols = tokens.shape[1]
    even = lax.rem(lax.axis_index("ns"), 2) == 0

    def column(c):
        north, south = jnp.where(even, ns1[c], ns0[c]), jnp.where(even, ns0[c], ns1[c])
        return jnp.concatenate([north[None], tokens[:, c], south[None]])

    return [swap(column(0), column(cols - 1), "ew", first) for first in range(2)]


def exchange(x):
    bands, strips = lax.axis_size("ns"), lax.axis_size("ew")
    if bands == WINDOW:
        return lax.all_to_all(x, ("ns", "ew"), 0, 0, tiled=True)
    inner = bands // WINDOW
    groups = [[a * inner + p for a in range(WINDOW)] for p in range(inner)]
    shape = x.shape
    x = x.reshape(WINDOW, strips, *shape[1:])
    x = lax.all_to_all(x, "ns", 0, 0, axis_index_groups=groups, tiled=True)
    x = lax.all_to_all(x, "ew", 1, 1, tiled=True)
    return x.reshape(shape)


def on_device(
    tokens,
    conv_gain,
    w_expand,
    dw_kernel,
    w_project,
    block_gain,
    block_qkv,
    block_out,
    grid_gain,
    grid_qkv,
    grid_out,
):
    rows, cols, channels = tokens.shape
    shares = WINDOW // lax.axis_size("ew")
    group = WINDOW * lax.axis_size("ew")
    across = cols // shares // WINDOW
    places = group // rows
    parts = across // places
    ns0, ns1 = [swap(tokens[0], tokens[rows - 1], "ns", first) for first in range(2)]
    own, moved = norm_own(tokens, conv_gain)
    tokens, own, moved = lax.optimization_barrier((tokens, own, moved))
    ew0, ew1 = swap_columns(tokens, ns0, ns1)
    sent = conv_and_windows(
        moved,
        own,
        (ns0, ns1, ew0, ew1),
        conv_gain,
        w_expand,
        dw_kernel,
        w_project,
        block_gain,
        block_qkv,
        block_out,
        rows,
        (places, shares, parts),
    )
    x = exchange(sent.reshape(group, -1, channels))
    y = grid_attention(x.reshape(-1, channels), grid_gain, grid_qkv, grid_out)
    returned = exchange(y.reshape(group, -1, channels)).reshape(rows, places, shares, parts, WINDOW, channels)
    return jnp.transpose(returned, (0, 2, 3, 1, 4, 5)).reshape(rows, cols, channels)


def solution(mesh):
    in_specs = (P("ns", "ew", None), P(), P(), P(), P(), P(), P(), P(), P(), P(), P())
    out_specs = P("ns", "ew", None)
    return jax.shard_map(
        on_device, mesh=mesh, in_specs=in_specs, out_specs=out_specs, check_vma=False
    )
```

```python
import functools
import math

import jax
import jax.numpy as jnp
from jax import lax
from jax.experimental import pallas as pl
from jax.experimental.pallas import tpu as pltpu
from jax.sharding import PartitionSpec as P

HEADS = 16
WINDOW = 8
FEATURES = 2048
LANES = 128
GROUP = 16
MIB = 1024 * 1024
NORM_LIMIT = 8
EDGE_LIMIT = 12
NORM_COST = 10_000_000_000
CONV_LIMIT = 32

NT = (((1,), (1,)), ((), ()))


def normalize(floats, scale_gain):
    center = floats - jnp.mean(floats, axis=-1, keepdims=True)
    spread = jnp.mean(center * center, axis=-1, keepdims=True)
    return center * lax.rsqrt(spread + 1e-05) * scale_gain


def gelu(v):
    inner = v * (math.sqrt(2 / math.pi) + (math.sqrt(2 / math.pi) * 0.044715) * (v * v))
    half = 0.5 * v
    return half + half * jnp.tanh(inner)


def tiles(value):
    return [value[:, t : t + LANES] for t in range(0, value.shape[1], LANES)]


def strided(ref, start, size, stride):
    return jnp.concatenate([ref[t, pl.ds(start, size, stride=stride), :] for t in range(ref.shape[0])], axis=1)


def by_place(tmp_ref, block, store):
    cols = block.shape[0]
    strips = cols // WINDOW
    for t, part in enumerate(tiles(block)):
        tmp_ref[t] = part
    for b in range(WINDOW):
        store(b * strips, strips, strided(tmp_ref, b, strips, WINDOW))


def norm_kernel(x_ref, gain_ref, normed_ref, moved_ref, tmp_ref):
    rows, cols, _ = x_ref.shape
    gain = gain_ref[...]
    for i in range(rows):

        block = x_ref[i].astype(jnp.float32)
        for out_ref, value in ((normed_ref, normalize(block, gain)), (moved_ref, block)):

            def store(at, count, part):
                out_ref[i * cols + at : i * cols + at + count, :] = part.astype(jnp.bfloat16)

            by_place(tmp_ref, value, store)


def norm_own(tokens, gain):
    rows, cols, channels = tokens.shape
    return pl.pallas_call(
        norm_kernel,
        out_shape=[jax.ShapeDtypeStruct((rows * cols, channels), jnp.bfloat16)] * 2,
        scratch_shapes=[pltpu.VMEM((channels // LANES, cols, LANES), jnp.float32)],
        compiler_params=pltpu.CompilerParams(vmem_limit_bytes=NORM_LIMIT * MIB),
        cost_estimate=pl.CostEstimate(flops=NORM_COST, bytes_accessed=4 * rows * cols * channels, transcendentals=0),
        name="norm_own",
    )(tokens, gain.reshape(1, channels))


def sorted_pair(first_ref, second_ref, axis):
    first, second = first_ref[...].astype(jnp.float32), second_ref[...].astype(jnp.float32)
    even = lax.rem(lax.axis_index(axis), 2) == 0
    return jnp.where(even, second, first), jnp.where(even, first, second)


def edge_kernel(ns0_ref, ns1_ref, gain_ref, w1_ref, out_ref, n_ref, tmp_ref):
    cols = ns0_ref.shape[0]
    gain = gain_ref[...]
    for k, block in enumerate(sorted_pair(ns0_ref, ns1_ref, "ns")):

        def store(at, count, part):
            n_ref[k * cols + at : k * cols + at + count, :] = part.astype(jnp.bfloat16)

        by_place(tmp_ref, normalize(block, gain), store)
    for k in range(2):
        normed = n_ref[k * cols : (k + 1) * cols, :]
        hidden = jnp.dot(normed, w1_ref[...], preferred_element_type=jnp.float32)
        out_ref[k] = gelu(hidden.astype(jnp.bfloat16)).reshape(out_ref.shape[1:])


def expand_edges(ns0, ns1, gain, w_expand):
    cols, channels = ns0.shape
    width = w_expand.shape[1]
    vmem = pl.BlockSpec(memory_space=pltpu.VMEM)
    return pl.pallas_call(
        edge_kernel,
        out_shape=jax.ShapeDtypeStruct((2, WINDOW, cols // WINDOW, width), jnp.bfloat16),
        in_specs=[vmem] * 4,
        out_specs=vmem,
        scratch_shapes=[
            pltpu.VMEM((2 * cols, channels), jnp.bfloat16),
            pltpu.VMEM((channels // LANES, cols, LANES), jnp.float32),
        ],
        compiler_params=pltpu.CompilerParams(vmem_limit_bytes=EDGE_LIMIT * MIB),
        cost_estimate=pl.CostEstimate(
            flops=4 * cols * channels * width,
            bytes_accessed=2 * channels * width + 4 * cols * (channels + width),
            transcendentals=2 * cols * width,
        ),
        name="expand_edges",
    )(ns0, ns1, gain.reshape(1, channels), w_expand)


def conv_kernel(
    conv_steps, shape, x_ref, own_ref, edge_ref, ew0_ref, ew1_ref, gain_ref, w1_ref, dw_ref, w2_ref,
    block_gain_ref, wqkv_ref, wout_ref, out_ref, n_ref, e_ref, acc_ref
):
    step = pl.program_id(0)
    tokens, channels = x_ref.shape
    rows = out_ref.shape[0]
    cols = tokens // rows
    strips = cols // WINDOW
    features = w1_ref.shape[1] // conv_steps
    side_rows = ew0_ref.shape[0]
    side_count = side_rows + -side_rows % 16

    @pl.when(step == 0)
    def _():
        gain = gain_ref[...]

        pad = jnp.zeros((side_count - side_rows, channels), jnp.float32)
        for k, block in enumerate(sorted_pair(ew0_ref, ew1_ref, "ew")):
            start = k * side_count
            n_ref[start : start + side_count, :] = normalize(
                jnp.concatenate([block, pad], axis=0), gain
            ).astype(jnp.bfloat16)
        for t in range(channels // LANES):
            acc_ref[t] = x_ref[:, t * LANES : (t + 1) * LANES].astype(jnp.float32)

    @pl.when(step < conv_steps)
    def _():
        block = pl.ds(pl.multiple_of(step * features, features), features)
        w1 = w1_ref[:, block]
        w2 = w2_ref[block, :]
        taps = [[dw_ref[a, b : b + 1, :].astype(jnp.bfloat16) for b in range(3)] for a in range(3)]

        def hidden(normed):
            return gelu(jnp.dot(normed, w1, preferred_element_type=jnp.float32).astype(jnp.bfloat16))

        sides = hidden(n_ref[...]).astype(jnp.float32)
        place_in_strip = lax.broadcasted_iota(jnp.int32, (strips, features), 0)
        for i in range(rows + 2):
            if i in (0, rows + 1):
                own = edge_ref[i // (rows + 1), :, :, block]
            else:
                own = hidden(own_ref[(i - 1) * cols : i * cols, :]).reshape(WINDOW, strips, features)
            e_ref[i, 1 : WINDOW + 1] = own
            last = pltpu.roll(own[WINDOW - 1].astype(jnp.float32), 1, axis=0)
            first = pltpu.roll(own[0].astype(jnp.float32), strips - 1, axis=0)
            low = jnp.where(place_in_strip == 0, sides[i : i + 1], last)
            high = jnp.where(place_in_strip == strips - 1, sides[side_count + i : side_count + i + 1], first)
            e_ref[i, 0] = low.astype(jnp.bfloat16)
            e_ref[i, WINDOW + 1] = high.astype(jnp.bfloat16)
        for i in range(rows):
            pieces = []
            for b in range(WINDOW):
                sums = []
                for da in range(3):
                    t = [e_ref[i + da, b + db] * taps[da][db] for db in range(3)]
                    sums.append(t[0] + t[1] + t[2])
                pieces.append(gelu(sums[0] + sums[1] + sums[2]))
            active = jnp.concatenate(pieces, axis=0)
            for t, part in enumerate(tiles(jnp.dot(active, w2, preferred_element_type=jnp.float32))):
                acc_ref[t, i * cols : (i + 1) * cols, :] += part

    @pl.when(step >= conv_steps)
    def _():
        places, across = shape
        _, all_places, shares, parts, side, _ = out_ref.shape
        size = rows * WINDOW
        first = (step - conv_steps) * places
        x = jnp.concatenate(
            [
                strided(acc_ref, share * across + part * all_places + first + j, size, strips)
                for j in range(places)
                for share in range(shares)
                for part in range(parts)
            ],
            axis=0,
        ).astype(jnp.bfloat16)
        result = attend_windows(x.astype(jnp.float32), block_gain_ref[...], wqkv_ref, wout_ref)
        result = result.astype(jnp.bfloat16).reshape(places, shares, parts, size // side, side, channels)
        for j in range(places):
            for share in range(shares):
                for part in range(parts):
                    out_ref[:, first + j, share, part] = result[j, share, part]


def conv_and_windows(moved, own, edges, ew0, ew1, gain, w_expand, dw_kernel, w_project, block_gain, w_qkv, w_out, rows, shape):
    tokens, channels = moved.shape
    cols = tokens // rows
    places, shares, parts = shape
    width = w_expand.shape[1]
    features = min(FEATURES, width)
    strips = cols // WINDOW
    conv_steps = width // features
    block_places = max(1, min(places, GROUP // (shares * parts)))
    side_rows = ew0.shape[0]
    side_count = side_rows + -side_rows % 16
    vmem = pl.BlockSpec(memory_space=pltpu.VMEM)
    return pl.pallas_call(
        functools.partial(conv_kernel, conv_steps, (block_places, strips // shares)),
        grid=(conv_steps + places // block_places,),
        out_shape=jax.ShapeDtypeStruct((rows, places, shares, parts, WINDOW, channels), jnp.bfloat16),
        in_specs=[
            *[vmem] * 5,
            vmem,
            vmem,
            pl.BlockSpec((3, 3, features), lambda step: (0, 0, jnp.minimum(step, conv_steps - 1))),
            vmem,
            vmem,
            vmem,
            vmem,
        ],
        out_specs=vmem,
        scratch_shapes=[
            pltpu.VMEM((2 * side_count, channels), jnp.bfloat16),
            pltpu.VMEM((rows + 2, WINDOW + 2, strips, features), jnp.bfloat16),
            pltpu.VMEM((channels // LANES, tokens, LANES), jnp.float32),
        ],
        compiler_params=pltpu.CompilerParams(dimension_semantics=("arbitrary",), vmem_limit_bytes=CONV_LIMIT * MIB),
        cost_estimate=pl.CostEstimate(
            flops=4 * tokens * channels * (width + 4 * channels),
            bytes_accessed=4 * channels * (width + 2 * channels) + 4 * tokens * channels,
            transcendentals=2 * tokens * width,
        ),
        name="conv_and_windows",
    )(
        moved,
        own,
        edges,
        ew0,
        ew1,
        gain.reshape(1, channels),
        w_expand,
        dw_kernel,
        w_project,
        block_gain.reshape(1, channels),
        w_qkv,
        w_out,
    )


def attend_windows(x, gain, wqkv_ref, wout_ref):
    tokens, channels = x.shape
    head_dim = channels // HEADS
    group = LANES // head_dim
    size = WINDOW * WINDOW
    two = 2 * head_dim
    pairs, groups = tokens // (2 * size), channels // LANES
    units = [(p, g) for p in range(pairs) for g in range(groups)]
    scale = math.log2(math.e) / math.sqrt(head_dim)
    normed = normalize(x, gain).astype(jnp.bfloat16)

    def project(first):
        return jnp.dot(normed, wqkv_ref[:, first : first + channels], preferred_element_type=jnp.float32)

    queries = (project(0) * scale).astype(jnp.bfloat16)
    keys = project(channels).astype(jnp.bfloat16)
    values = lax.dot_general(
        wqkv_ref[:, 2 * channels :].T, normed, NT, preferred_element_type=jnp.float32
    ).astype(jnp.bfloat16)
    lane = lax.broadcasted_iota(jnp.int32, (1, LANES), 1)
    head_lanes = [(lane // head_dim == h).astype(jnp.float32).astype(jnp.bfloat16) for h in range(group)]
    halves = [(lane // size == h).astype(jnp.float32).astype(jnp.bfloat16) for h in range(2)]
    pick = (
        (
            lax.broadcasted_iota(jnp.int32, (size, 2 * size), 0)
            == lax.broadcasted_iota(jnp.int32, (size, 2 * size), 1) % size
        )
        .astype(jnp.float32)
        .astype(jnp.bfloat16)
    )
    scores = {}
    for p, g in units:
        for odd in range(2):
            at = (2 * p + odd) * size
            q = queries[at : at + size, g * LANES : (g + 1) * LANES]
            k = keys[at : at + size, g * LANES : (g + 1) * LANES]
            q_heads = jnp.concatenate([q * m for m in head_lanes], axis=0)
            scores[p, g, odd] = lax.dot_general(k, q_heads, NT, preferred_element_type=jnp.float32)
    weights = {}
    for unit, s in scores.items():
        raised = jnp.exp2(s - jnp.max(s, axis=0, keepdims=True))
        weights[unit] = (raised * (1.0 / jnp.sum(raised, axis=0, keepdims=True))).astype(jnp.bfloat16)
    mixed = {}
    for p, g in units:
        both = jnp.concatenate([weights[p, g, 0], weights[p, g, 1]], axis=0)
        for t in range(group // 2):
            at = g * LANES + t * two
            v = values[at : at + two, p * 2 * size : (p + 1) * 2 * size]
            v_halves = jnp.concatenate([v * m for m in halves], axis=0)
            mixed[p, g, t] = jnp.dot(
                v_halves, both[:, t * 2 * size : (t + 1) * 2 * size], preferred_element_type=jnp.float32
            ).astype(jnp.bfloat16)
    parts = {}
    for p, g in units:
        own = [
            mixed[p, g, t][odd * two + h * head_dim : odd * two + (h + 1) * head_dim] * halves[h]
            for odd in range(2)
            for t in range(group // 2)
            for h in range(2)
        ]
        parts[p, g] = lax.dot_general(
            pick, jnp.concatenate(own, axis=0), NT, preferred_element_type=jnp.float32
        ).astype(jnp.bfloat16)
    blended = [
        jnp.concatenate([parts[p, g][:, odd * LANES : (odd + 1) * LANES] for g in range(groups)], axis=1)
        for p in range(pairs)
        for odd in range(2)
    ]
    return x + jnp.dot(jnp.concatenate(blended, axis=0), wout_ref[...], preferred_element_type=jnp.float32)


def grid_kernel(x_ref, gain_ref, wqkv_ref, wout_ref, out_ref, floats_ref):
    step = pl.program_id(0)
    tokens, channels = x_ref.shape
    size = WINDOW * WINDOW
    windows = tokens // size
    block = windows // pl.num_programs(0)

    @pl.when(step == 0)
    def _():
        for t, part in enumerate(tiles(x_ref[...])):
            floats_ref[t] = part.astype(jnp.float32)

    first = step * block
    x = jnp.concatenate([strided(floats_ref, first + w, size, windows) for w in range(block)], axis=0)
    result = attend_windows(x, gain_ref[...], wqkv_ref, wout_ref)
    for t, part in enumerate(tiles(result)):
        for w in range(block):
            floats_ref[t, pl.ds(first + w, size, stride=windows), :] = part[w * size : (w + 1) * size]

    @pl.when(step == pl.num_programs(0) - 1)
    def _():
        for t in range(floats_ref.shape[0]):
            out_ref[:, t * LANES : (t + 1) * LANES] = floats_ref[t].astype(jnp.bfloat16)


def grid_attention(x, gain, w_qkv, w_out):
    tokens, channels = x.shape
    windows = tokens // (WINDOW * WINDOW)
    vmem = pl.BlockSpec(memory_space=pltpu.VMEM)
    return pl.pallas_call(
        grid_kernel,
        grid=(windows // min(GROUP, windows),),
        out_shape=jax.ShapeDtypeStruct((tokens, channels), jnp.bfloat16),
        in_specs=[vmem] * 4,
        out_specs=vmem,
        scratch_shapes=[pltpu.VMEM((channels // LANES, tokens, LANES), jnp.float32)],
        compiler_params=pltpu.CompilerParams(dimension_semantics=("arbitrary",), vmem_limit_bytes=24 * MIB),
        cost_estimate=pl.CostEstimate(
            flops=16 * tokens * channels * channels,
            bytes_accessed=8 * channels * channels + 4 * tokens * channels,
            transcendentals=HEADS * tokens * WINDOW * WINDOW,
        ),
        name="grid_attention",
    )(x, gain.reshape(1, channels), w_qkv, w_out)


def swap(low_edge, high_edge, axis, first):
    pairs = [(a, a + 1) for a in range(first, lax.axis_size(axis) - 1, 2)]
    lower = lax.rem(lax.axis_index(axis), 2) == first
    return lax.ppermute(
        jnp.where(lower, high_edge, low_edge), axis, pairs + [(target, source) for source, target in pairs]
    )


def swap_columns(tokens, corners0, corners1):
    even = lax.rem(lax.axis_index("ns"), 2) == 0

    def column(c, k):
        north, south = jnp.where(even, corners1[k], corners0[k]), jnp.where(even, corners0[k], corners1[k])
        return jnp.concatenate([north[None], tokens[:, c], south[None]])

    low, high = column(0, 0), column(tokens.shape[1] - 1, 1)
    return [swap(low, high, "ew", first) for first in range(2)]


def exchange(x):
    bands, strips = lax.axis_size("ns"), lax.axis_size("ew")
    if bands == WINDOW:
        return lax.all_to_all(x, ("ns", "ew"), 0, 0, tiled=True)
    inner = bands // WINDOW
    groups = [[a * inner + p for a in range(WINDOW)] for p in range(inner)]
    shape = x.shape
    x = x.reshape(WINDOW, strips, *shape[1:])
    x = lax.all_to_all(x, "ns", 0, 0, axis_index_groups=groups, tiled=True)
    x = lax.all_to_all(x, "ew", 1, 1, tiled=True)
    return x.reshape(shape)


def on_device(
    tokens,
    conv_gain,
    w_expand,
    dw_kernel,
    w_project,
    block_gain,
    block_qkv,
    block_out,
    grid_gain,
    grid_qkv,
    grid_out,
):
    rows, cols, channels = tokens.shape
    shares = WINDOW // lax.axis_size("ew")
    group = WINDOW * lax.axis_size("ew")
    across = cols // shares // WINDOW
    places = group // rows
    parts = across // places
    ns0, ns1 = [swap(tokens[0], tokens[rows - 1], "ns", first) for first in range(2)]
    own, moved = norm_own(tokens, conv_gain)
    corners = [jnp.concatenate([ns[:1], ns[cols - 1 :]]) for ns in (ns0, ns1)]
    corners, own, moved = lax.optimization_barrier((corners, own, moved))
    ew0, ew1 = swap_columns(tokens, *corners)
    sent = conv_and_windows(
        moved,
        own,
        expand_edges(ns0, ns1, conv_gain, w_expand),
        ew0,
        ew1,
        conv_gain,
        w_expand,
        dw_kernel,
        w_project,
        block_gain,
        block_qkv,
        block_out,
        rows,
        (places, shares, parts),
    )
    x = exchange(sent.reshape(group, -1, channels))
    y = grid_attention(x.reshape(-1, channels), grid_gain, grid_qkv, grid_out)
    returned = exchange(y.reshape(group, -1, channels)).reshape(rows, places, shares, parts, WINDOW, channels)
    return jnp.transpose(returned, (0, 2, 3, 1, 4, 5)).reshape(rows, cols, channels)


def solution(mesh):
    in_specs = (P("ns", "ew", None), P(), P(), P(), P(), P(), P(), P(), P(), P(), P())
    out_specs = P("ns", "ew", None)
    return jax.shard_map(
        on_device, mesh=mesh, in_specs=in_specs, out_specs=out_specs, check_vma=False
    )
```

```python
import functools
import math

import jax
import jax.numpy as jnp
from jax import lax
from jax.experimental import pallas as pl
from jax.experimental.pallas import tpu as pltpu
from jax.sharding import PartitionSpec as P

HEADS = 16
WINDOW = 8
FEATURES = 2048
LANES = 128
GROUP = 16
MIB = 1024 * 1024
NORM_LIMIT = 8
EDGE_LIMIT = 12
NORM_COST = 10_000_000_000
CONV_LIMIT = 32

NT = (((1,), (1,)), ((), ()))


def normalize(floats, scale_gain):
    center = floats - jnp.mean(floats, axis=-1, keepdims=True)
    spread = jnp.mean(center * center, axis=-1, keepdims=True)
    return center * lax.rsqrt(spread + 1e-05) * scale_gain


def gelu(v):
    inner = v * (math.sqrt(2 / math.pi) + (math.sqrt(2 / math.pi) * 0.044715) * (v * v))
    half = 0.5 * v
    return half + half * jnp.tanh(inner)


def tiles(value):
    return [value[:, t : t + LANES] for t in range(0, value.shape[1], LANES)]


def strided(ref, start, size, stride):
    return jnp.concatenate([ref[t, pl.ds(start, size, stride=stride), :] for t in range(ref.shape[0])], axis=1)


def by_place(tmp_ref, block, store):
    cols = block.shape[0]
    strips = cols // WINDOW
    for t, part in enumerate(tiles(block)):
        tmp_ref[t] = part
    for b in range(WINDOW):
        store(b * strips, strips, strided(tmp_ref, b, strips, WINDOW))


def norm_kernel(x_ref, gain_ref, normed_ref, moved_ref, tmp_ref):
    rows, cols, _ = x_ref.shape
    gain = gain_ref[...]
    for i in range(rows):

        block = x_ref[i].astype(jnp.float32)
        for out_ref, value in ((normed_ref, normalize(block, gain)), (moved_ref, block)):

            def store(at, count, part):
                out_ref[i * cols + at : i * cols + at + count, :] = part.astype(jnp.bfloat16)

            by_place(tmp_ref, value, store)


def norm_own(tokens, gain):
    rows, cols, channels = tokens.shape
    return pl.pallas_call(
        norm_kernel,
        out_shape=[jax.ShapeDtypeStruct((rows * cols, channels), jnp.bfloat16)] * 2,
        scratch_shapes=[pltpu.VMEM((channels // LANES, cols, LANES), jnp.float32)],
        compiler_params=pltpu.CompilerParams(vmem_limit_bytes=NORM_LIMIT * MIB),
        cost_estimate=pl.CostEstimate(flops=NORM_COST, bytes_accessed=4 * rows * cols * channels, transcendentals=0),
        name="norm_own",
    )(tokens, gain.reshape(1, channels))


def sorted_pair(first_ref, second_ref, axis):
    first, second = first_ref[...].astype(jnp.float32), second_ref[...].astype(jnp.float32)
    even = lax.rem(lax.axis_index(axis), 2) == 0
    return jnp.where(even, second, first), jnp.where(even, first, second)


def edge_kernel(ns0_ref, ns1_ref, gain_ref, w1_ref, out_ref, n_ref, tmp_ref):
    cols = ns0_ref.shape[0]
    gain = gain_ref[...]
    for k, block in enumerate(sorted_pair(ns0_ref, ns1_ref, "ns")):

        def store(at, count, part):
            n_ref[k * cols + at : k * cols + at + count, :] = part.astype(jnp.bfloat16)

        by_place(tmp_ref, normalize(block, gain), store)
    for k in range(2):
        normed = n_ref[k * cols : (k + 1) * cols, :]
        hidden = jnp.dot(normed, w1_ref[...], preferred_element_type=jnp.float32)
        out_ref[k] = gelu(hidden.astype(jnp.bfloat16)).reshape(out_ref.shape[1:])


def expand_edges(ns0, ns1, gain, w_expand):
    cols, channels = ns0.shape
    width = w_expand.shape[1]
    vmem = pl.BlockSpec(memory_space=pltpu.VMEM)
    return pl.pallas_call(
        edge_kernel,
        out_shape=jax.ShapeDtypeStruct((2, WINDOW, cols // WINDOW, width), jnp.bfloat16),
        in_specs=[vmem] * 4,
        out_specs=vmem,
        scratch_shapes=[
            pltpu.VMEM((2 * cols, channels), jnp.bfloat16),
            pltpu.VMEM((channels // LANES, cols, LANES), jnp.float32),
        ],
        compiler_params=pltpu.CompilerParams(vmem_limit_bytes=EDGE_LIMIT * MIB),
        cost_estimate=pl.CostEstimate(
            flops=4 * cols * channels * width,
            bytes_accessed=2 * channels * width + 4 * cols * (channels + width),
            transcendentals=2 * cols * width,
        ),
        name="expand_edges",
    )(ns0, ns1, gain.reshape(1, channels), w_expand)


def conv_kernel(
    conv_steps, shape, x_ref, own_ref, edge_ref, ew0_ref, ew1_ref, gain_ref, w1_ref, dw_ref, w2_ref,
    block_gain_ref, wqkv_ref, wout_ref, out_ref, n_ref, e_ref, acc_ref
):
    step = pl.program_id(0)
    tokens, channels = x_ref.shape
    rows = out_ref.shape[0]
    cols = tokens // rows
    strips = cols // WINDOW
    features = w1_ref.shape[1] // conv_steps
    side_rows = ew0_ref.shape[0]
    side_count = side_rows + -side_rows % 16

    @pl.when(step == 0)
    def _():
        gain = gain_ref[...]

        pad = jnp.zeros((side_count - side_rows, channels), jnp.float32)
        for k, block in enumerate(sorted_pair(ew0_ref, ew1_ref, "ew")):
            start = k * side_count
            n_ref[start : start + side_count, :] = normalize(
                jnp.concatenate([block, pad], axis=0), gain
            ).astype(jnp.bfloat16)
        for t in range(channels // LANES):
            acc_ref[t] = x_ref[:, t * LANES : (t + 1) * LANES].astype(jnp.float32)

    @pl.when(step < conv_steps)
    def _():
        block = pl.ds(pl.multiple_of(step * features, features), features)
        w1 = w1_ref[:, block]
        w2 = w2_ref[block, :]
        taps = [[dw_ref[a, b : b + 1, :].astype(jnp.bfloat16) for b in range(3)] for a in range(3)]

        def hidden(normed):
            return gelu(jnp.dot(normed, w1, preferred_element_type=jnp.float32).astype(jnp.bfloat16))

        sides = hidden(n_ref[...]).astype(jnp.float32)
        place_in_strip = lax.broadcasted_iota(jnp.int32, (strips, features), 0)
        for i in range(rows + 2):
            if i in (0, rows + 1):
                own = edge_ref[i // (rows + 1), :, :, block]
            else:
                own = hidden(own_ref[(i - 1) * cols : i * cols, :]).reshape(WINDOW, strips, features)
            e_ref[i, 1 : WINDOW + 1] = own
            last = pltpu.roll(own[WINDOW - 1].astype(jnp.float32), 1, axis=0)
            first = pltpu.roll(own[0].astype(jnp.float32), strips - 1, axis=0)
            low = jnp.where(place_in_strip == 0, sides[i : i + 1], last)
            high = jnp.where(place_in_strip == strips - 1, sides[side_count + i : side_count + i + 1], first)
            e_ref[i, 0] = low.astype(jnp.bfloat16)
            e_ref[i, WINDOW + 1] = high.astype(jnp.bfloat16)
        for i in range(rows):
            pieces = []
            for b in range(WINDOW):
                sums = []
                for da in range(3):
                    t = [e_ref[i + da, b + db] * taps[da][db] for db in range(3)]
                    sums.append(t[0] + t[1] + t[2])
                pieces.append(gelu(sums[0] + sums[1] + sums[2]))
            active = jnp.concatenate(pieces, axis=0)
            for t, part in enumerate(tiles(jnp.dot(active, w2, preferred_element_type=jnp.float32))):
                acc_ref[t, i * cols : (i + 1) * cols, :] += part

    @pl.when(step >= conv_steps)
    def _():
        places, across = shape
        _, all_places, shares, parts, side, _ = out_ref.shape
        size = rows * WINDOW
        first = (step - conv_steps) * places
        x = jnp.concatenate(
            [
                strided(acc_ref, share * across + part * all_places + first + j, size, strips)
                for j in range(places)
                for share in range(shares)
                for part in range(parts)
            ],
            axis=0,
        ).astype(jnp.bfloat16)
        result = attend_windows(x.astype(jnp.float32), block_gain_ref[...], wqkv_ref, wout_ref)
        result = result.astype(jnp.bfloat16).reshape(places, shares, parts, size // side, side, channels)
        for j in range(places):
            for share in range(shares):
                for part in range(parts):
                    out_ref[:, first + j, share, part] = result[j, share, part]


def conv_and_windows(moved, own, edges, ew0, ew1, gain, w_expand, dw_kernel, w_project, block_gain, w_qkv, w_out, rows, shape):
    tokens, channels = moved.shape
    cols = tokens // rows
    places, shares, parts = shape
    width = w_expand.shape[1]
    features = min(FEATURES, width)
    strips = cols // WINDOW
    conv_steps = width // features
    block_places = max(1, min(places, GROUP // (shares * parts)))
    side_rows = ew0.shape[0]
    side_count = side_rows + -side_rows % 16
    vmem = pl.BlockSpec(memory_space=pltpu.VMEM)
    return pl.pallas_call(
        functools.partial(conv_kernel, conv_steps, (block_places, strips // shares)),
        grid=(conv_steps + places // block_places,),
        out_shape=jax.ShapeDtypeStruct((rows, places, shares, parts, WINDOW, channels), jnp.bfloat16),
        in_specs=[
            *[vmem] * 5,
            vmem,
            vmem,
            pl.BlockSpec((3, 3, features), lambda step: (0, 0, jnp.minimum(step, conv_steps - 1))),
            vmem,
            vmem,
            vmem,
            vmem,
        ],
        out_specs=vmem,
        scratch_shapes=[
            pltpu.VMEM((2 * side_count, channels), jnp.bfloat16),
            pltpu.VMEM((rows + 2, WINDOW + 2, strips, features), jnp.bfloat16),
            pltpu.VMEM((channels // LANES, tokens, LANES), jnp.float32),
        ],
        compiler_params=pltpu.CompilerParams(dimension_semantics=("arbitrary",), vmem_limit_bytes=CONV_LIMIT * MIB),
        cost_estimate=pl.CostEstimate(
            flops=4 * tokens * channels * (width + 4 * channels),
            bytes_accessed=4 * channels * (width + 2 * channels) + 4 * tokens * channels,
            transcendentals=2 * tokens * width,
        ),
        name="conv_and_windows",
    )(
        moved,
        own,
        edges,
        ew0,
        ew1,
        gain.reshape(1, channels),
        w_expand,
        dw_kernel,
        w_project,
        block_gain.reshape(1, channels),
        w_qkv,
        w_out,
    )


def attend_windows(x, gain, wqkv_ref, wout_ref):
    tokens, channels = x.shape
    head_dim = channels // HEADS
    group = LANES // head_dim
    size = WINDOW * WINDOW
    two = 2 * head_dim
    pairs, groups = tokens // (2 * size), channels // LANES
    units = [(p, g) for p in range(pairs) for g in range(groups)]
    scale = math.log2(math.e) / math.sqrt(head_dim)
    normed = normalize(x, gain).astype(jnp.bfloat16)

    def project(first):
        return jnp.dot(normed, wqkv_ref[:, first : first + channels], preferred_element_type=jnp.float32)

    queries = lax.dot_general(wqkv_ref[:, :channels].T, normed, NT, preferred_element_type=jnp.float32) * scale
    keys = project(channels).astype(jnp.bfloat16)
    values = lax.dot_general(
        wqkv_ref[:, 2 * channels :].T, normed, NT, preferred_element_type=jnp.float32
    ).astype(jnp.bfloat16)
    lane = lax.broadcasted_iota(jnp.int32, (1, LANES), 1)
    halves = [(lane // size == h).astype(jnp.float32).astype(jnp.bfloat16) for h in range(2)]
    scores = {}
    zeros = jnp.zeros((two, 2 * size), jnp.bfloat16)
    for p, g in units:
        own = queries[g * LANES : (g + 1) * LANES, p * 2 * size : (p + 1) * 2 * size]
        turned = pltpu.roll(own, size, axis=1).astype(jnp.bfloat16)
        own = own.astype(jnp.bfloat16)
        for odd in range(2):
            at = (2 * p + odd) * size
            k = keys[at : at + size, g * LANES : (g + 1) * LANES]
            columns = []
            for t in range(group // 2):
                heads = []
                for h in range(2):
                    source = own if h == odd else turned
                    row = t * two + h * head_dim
                    heads.append(source[row : row + head_dim] * halves[h])
                column = [zeros] * (group // 2)
                column[t] = jnp.concatenate(heads, axis=0)
                columns.append(jnp.concatenate(column, axis=0))
            scores[p, g, odd] = jnp.dot(k, jnp.concatenate(columns, axis=1), preferred_element_type=jnp.float32)
    weights = {}
    for unit, s in scores.items():
        raised = jnp.exp2(s - jnp.max(s, axis=0, keepdims=True))
        weights[unit] = (raised * (1.0 / jnp.sum(raised, axis=0, keepdims=True))).astype(jnp.bfloat16)
    mixed = {}
    for p, g in units:
        both = jnp.concatenate([weights[p, g, 0], weights[p, g, 1]], axis=0)
        for t in range(group // 2):
            at = g * LANES + t * two
            v = values[at : at + two, p * 2 * size : (p + 1) * 2 * size]
            v_halves = jnp.concatenate([v * m for m in halves], axis=0)
            mixed[p, g, t] = jnp.dot(
                v_halves, both[:, t * 2 * size : (t + 1) * 2 * size], preferred_element_type=jnp.float32
            )
    even_head = lane // head_dim % 2 == 0
    blended = []
    for p in range(pairs):
        for odd in range(2):
            parts = []
            for g in range(groups):
                turned = jnp.concatenate(
                    [mixed[p, g, t][odd * two : (odd + 1) * two] for t in range(group // 2)], axis=0
                ).T
                parts.append(jnp.where(even_head, turned[:size], turned[size:]).astype(jnp.bfloat16))
            blended.append(jnp.concatenate(parts, axis=1))
    return x + jnp.dot(jnp.concatenate(blended, axis=0), wout_ref[...], preferred_element_type=jnp.float32)


def grid_kernel(x_ref, gain_ref, wqkv_ref, wout_ref, out_ref, floats_ref):
    step = pl.program_id(0)
    tokens, channels = x_ref.shape
    size = WINDOW * WINDOW
    windows = tokens // size
    block = windows // pl.num_programs(0)

    @pl.when(step == 0)
    def _():
        for t, part in enumerate(tiles(x_ref[...])):
            floats_ref[t] = part.astype(jnp.float32)

    first = step * block
    x = jnp.concatenate([strided(floats_ref, first + w, size, windows) for w in range(block)], axis=0)
    result = attend_windows(x, gain_ref[...], wqkv_ref, wout_ref)
    for t, part in enumerate(tiles(result)):
        for w in range(block):
            floats_ref[t, pl.ds(first + w, size, stride=windows), :] = part[w * size : (w + 1) * size]

    @pl.when(step == pl.num_programs(0) - 1)
    def _():
        for t in range(floats_ref.shape[0]):
            out_ref[:, t * LANES : (t + 1) * LANES] = floats_ref[t].astype(jnp.bfloat16)


def grid_attention(x, gain, w_qkv, w_out):
    tokens, channels = x.shape
    windows = tokens // (WINDOW * WINDOW)
    vmem = pl.BlockSpec(memory_space=pltpu.VMEM)
    return pl.pallas_call(
        grid_kernel,
        grid=(windows // min(GROUP, windows),),
        out_shape=jax.ShapeDtypeStruct((tokens, channels), jnp.bfloat16),
        in_specs=[vmem] * 4,
        out_specs=vmem,
        scratch_shapes=[pltpu.VMEM((channels // LANES, tokens, LANES), jnp.float32)],
        compiler_params=pltpu.CompilerParams(dimension_semantics=("arbitrary",), vmem_limit_bytes=24 * MIB),
        cost_estimate=pl.CostEstimate(
            flops=16 * tokens * channels * channels,
            bytes_accessed=8 * channels * channels + 4 * tokens * channels,
            transcendentals=HEADS * tokens * WINDOW * WINDOW,
        ),
        name="grid_attention",
    )(x, gain.reshape(1, channels), w_qkv, w_out)


def swap(low_edge, high_edge, axis, first):
    pairs = [(a, a + 1) for a in range(first, lax.axis_size(axis) - 1, 2)]
    lower = lax.rem(lax.axis_index(axis), 2) == first
    return lax.ppermute(
        jnp.where(lower, high_edge, low_edge), axis, pairs + [(target, source) for source, target in pairs]
    )


def swap_columns(tokens, corners0, corners1):
    even = lax.rem(lax.axis_index("ns"), 2) == 0

    def column(c, k):
        north, south = jnp.where(even, corners1[k], corners0[k]), jnp.where(even, corners0[k], corners1[k])
        return jnp.concatenate([north[None], tokens[:, c], south[None]])

    low, high = column(0, 0), column(tokens.shape[1] - 1, 1)
    return [swap(low, high, "ew", first) for first in range(2)]


def exchange(x):
    bands, strips = lax.axis_size("ns"), lax.axis_size("ew")
    if bands == WINDOW:
        return lax.all_to_all(x, ("ns", "ew"), 0, 0, tiled=True)
    inner = bands // WINDOW
    groups = [[a * inner + p for a in range(WINDOW)] for p in range(inner)]
    shape = x.shape
    x = x.reshape(WINDOW, strips, *shape[1:])
    x = lax.all_to_all(x, "ns", 0, 0, axis_index_groups=groups, tiled=True)
    x = lax.all_to_all(x, "ew", 1, 1, tiled=True)
    return x.reshape(shape)


def on_device(
    tokens,
    conv_gain,
    w_expand,
    dw_kernel,
    w_project,
    block_gain,
    block_qkv,
    block_out,
    grid_gain,
    grid_qkv,
    grid_out,
):
    rows, cols, channels = tokens.shape
    shares = WINDOW // lax.axis_size("ew")
    group = WINDOW * lax.axis_size("ew")
    across = cols // shares // WINDOW
    places = group // rows
    parts = across // places
    ns0, ns1 = [swap(tokens[0], tokens[rows - 1], "ns", first) for first in range(2)]
    own, moved = norm_own(tokens, conv_gain)
    corners = [jnp.concatenate([ns[:1], ns[cols - 1 :]]) for ns in (ns0, ns1)]
    corners, own, moved = lax.optimization_barrier((corners, own, moved))
    ew0, ew1 = swap_columns(tokens, *corners)
    sent = conv_and_windows(
        moved,
        own,
        expand_edges(ns0, ns1, conv_gain, w_expand),
        ew0,
        ew1,
        conv_gain,
        w_expand,
        dw_kernel,
        w_project,
        block_gain,
        block_qkv,
        block_out,
        rows,
        (places, shares, parts),
    )
    x = exchange(sent.reshape(group, -1, channels))
    y = grid_attention(x.reshape(-1, channels), grid_gain, grid_qkv, grid_out)
    returned = exchange(y.reshape(group, -1, channels)).reshape(rows, places, shares, parts, WINDOW, channels)
    return jnp.transpose(returned, (0, 2, 3, 1, 4, 5)).reshape(rows, cols, channels)


def solution(mesh):
    in_specs = (P("ns", "ew", None), P(), P(), P(), P(), P(), P(), P(), P(), P(), P())
    out_specs = P("ns", "ew", None)
    return jax.shard_map(
        on_device, mesh=mesh, in_specs=in_specs, out_specs=out_specs, check_vma=False
    )
```

```python
import functools
import math

import jax
import jax.numpy as jnp
from jax import lax
from jax.experimental import pallas as pl
from jax.experimental.pallas import tpu as pltpu
from jax.sharding import PartitionSpec as P

HEADS = 16
WINDOW = 8
FEATURES = 2048
LANES = 128
GROUP = 16
MIB = 1024 * 1024
NORM_LIMIT = 8
EDGE_LIMIT = 12
NORM_COST = 10_000_000_000
CONV_LIMIT = 32

NT = (((1,), (1,)), ((), ()))


def normalize(floats, scale_gain):
    center = floats - jnp.mean(floats, axis=-1, keepdims=True)
    spread = jnp.mean(center * center, axis=-1, keepdims=True)
    return center * lax.rsqrt(spread + 1e-05) * scale_gain


def gelu_of_double(half):
    root = math.sqrt(2 / math.pi)
    inner = half * (2 * root + (8 * root * 0.044715) * (half * half))
    return half + half * jnp.tanh(inner)


def tiles(value):
    return [value[:, t : t + LANES] for t in range(0, value.shape[1], LANES)]


def strided(ref, start, size, stride):
    return jnp.concatenate([ref[t, pl.ds(start, size, stride=stride), :] for t in range(ref.shape[0])], axis=1)


def by_place(tmp_ref, block, store):
    cols = block.shape[0]
    strips = cols // WINDOW
    for t, part in enumerate(tiles(block)):
        tmp_ref[t, :cols] = part
    for b in range(WINDOW):
        store(b * strips, strips, strided(tmp_ref, b, strips, WINDOW))


def norm_kernel(x_ref, gain_ref, normed_ref, moved_ref, tmp_ref):
    rows, cols, _ = x_ref.shape
    gain = 0.5 * gain_ref[...]
    for i in range(rows):

        block = x_ref[i].astype(jnp.float32)
        for out_ref, value in ((normed_ref, normalize(block, gain)), (moved_ref, block)):

            def store(at, count, part):
                out_ref[i * cols + at : i * cols + at + count, :] = part.astype(jnp.bfloat16)

            by_place(tmp_ref, value, store)


def norm_own(tokens, gain):
    rows, cols, channels = tokens.shape
    return pl.pallas_call(
        norm_kernel,
        out_shape=[jax.ShapeDtypeStruct((rows * cols, channels), jnp.bfloat16)] * 2,
        scratch_shapes=[pltpu.VMEM((channels // LANES, cols + WINDOW, LANES), jnp.float32)],
        compiler_params=pltpu.CompilerParams(vmem_limit_bytes=NORM_LIMIT * MIB),
        cost_estimate=pl.CostEstimate(flops=NORM_COST, bytes_accessed=4 * rows * cols * channels, transcendentals=0),
        name="norm_own",
    )(tokens, gain.reshape(1, channels))


def sorted_pair(first_ref, second_ref, axis):
    first, second = first_ref[...].astype(jnp.float32), second_ref[...].astype(jnp.float32)
    even = lax.rem(lax.axis_index(axis), 2) == 0
    return jnp.where(even, second, first), jnp.where(even, first, second)


def edge_kernel(ns0_ref, ns1_ref, gain_ref, w1_ref, out_ref, n_ref, tmp_ref):
    cols = ns0_ref.shape[0]
    gain = 0.5 * gain_ref[...]
    for k, block in enumerate(sorted_pair(ns0_ref, ns1_ref, "ns")):

        def store(at, count, part):
            n_ref[k * cols + at : k * cols + at + count, :] = part.astype(jnp.bfloat16)

        by_place(tmp_ref, normalize(block, gain), store)
    for k in range(2):
        normed = n_ref[k * cols : (k + 1) * cols, :]
        hidden = jnp.dot(normed, w1_ref[...], preferred_element_type=jnp.float32)
        out_ref[k] = gelu_of_double(hidden.astype(jnp.bfloat16)).reshape(out_ref.shape[1:])


def expand_edges(ns0, ns1, gain, w_expand):
    cols, channels = ns0.shape
    width = w_expand.shape[1]
    vmem = pl.BlockSpec(memory_space=pltpu.VMEM)
    return pl.pallas_call(
        edge_kernel,
        out_shape=jax.ShapeDtypeStruct((2, WINDOW, cols // WINDOW, width), jnp.bfloat16),
        in_specs=[vmem] * 4,
        out_specs=vmem,
        scratch_shapes=[
            pltpu.VMEM((2 * cols, channels), jnp.bfloat16),
            pltpu.VMEM((channels // LANES, cols + WINDOW, LANES), jnp.float32),
        ],
        compiler_params=pltpu.CompilerParams(vmem_limit_bytes=EDGE_LIMIT * MIB),
        cost_estimate=pl.CostEstimate(
            flops=4 * cols * channels * width,
            bytes_accessed=2 * channels * width + 4 * cols * (channels + width),
            transcendentals=2 * cols * width,
        ),
        name="expand_edges",
    )(ns0, ns1, gain.reshape(1, channels), w_expand)


def conv_kernel(
    conv_steps, shape, x_ref, own_ref, edge_ref, ew0_ref, ew1_ref, gain_ref, w1_ref, dw_ref, w2_ref,
    block_gain_ref, wqkv_ref, wout_ref, out_ref, n_ref, e_ref, acc_ref
):
    step = pl.program_id(0)
    tokens, channels = x_ref.shape
    rows = out_ref.shape[0]
    cols = tokens // rows
    strips = cols // WINDOW
    features = w1_ref.shape[1] // conv_steps
    side_rows = ew0_ref.shape[0]
    side_count = side_rows + -side_rows % 16

    @pl.when(step == 0)
    def _():
        gain = 0.5 * gain_ref[...]

        pad = jnp.zeros((side_count - side_rows, channels), jnp.float32)
        for k, block in enumerate(sorted_pair(ew0_ref, ew1_ref, "ew")):
            start = k * side_count
            n_ref[start : start + side_count, :] = normalize(
                jnp.concatenate([block, pad], axis=0), gain
            ).astype(jnp.bfloat16)
        for t in range(channels // LANES):
            acc_ref[t, :tokens] = x_ref[:, t * LANES : (t + 1) * LANES].astype(jnp.float32)

    @pl.when(step < conv_steps)
    def _():
        block = pl.ds(pl.multiple_of(step * features, features), features)
        w1 = w1_ref[:, block]
        w2 = w2_ref[block, :]
        taps = [[(0.5 * dw_ref[a, b : b + 1, :]).astype(jnp.bfloat16) for b in range(3)] for a in range(3)]

        def hidden(normed):
            return gelu_of_double(jnp.dot(normed, w1, preferred_element_type=jnp.float32).astype(jnp.bfloat16))

        sides = hidden(n_ref[...]).astype(jnp.float32)
        place_in_strip = lax.broadcasted_iota(jnp.int32, (strips, features), 0)
        for i in range(rows + 2):
            if i in (0, rows + 1):
                own = edge_ref[i // (rows + 1), :, :, block]
            else:
                own = hidden(own_ref[(i - 1) * cols : i * cols, :]).reshape(WINDOW, strips, features)
            e_ref[i, 1 : WINDOW + 1] = own
            last = pltpu.roll(own[WINDOW - 1].astype(jnp.float32), 1, axis=0)
            first = pltpu.roll(own[0].astype(jnp.float32), strips - 1, axis=0)
            low = jnp.where(place_in_strip == 0, sides[i : i + 1], last)
            high = jnp.where(place_in_strip == strips - 1, sides[side_count + i : side_count + i + 1], first)
            e_ref[i, 0] = low.astype(jnp.bfloat16)
            e_ref[i, WINDOW + 1] = high.astype(jnp.bfloat16)
        for i in range(rows):
            pieces = []
            for b in range(WINDOW):
                sums = []
                for da in range(3):
                    t = [e_ref[i + da, b + db] * taps[da][db] for db in range(3)]
                    sums.append(t[0] + t[1] + t[2])
                pieces.append(gelu_of_double(sums[0] + sums[1] + sums[2]))
            active = jnp.concatenate(pieces, axis=0)
            for t, part in enumerate(tiles(jnp.dot(active, w2, preferred_element_type=jnp.float32))):
                acc_ref[t, i * cols : (i + 1) * cols, :] += part

    @pl.when(step >= conv_steps)
    def _():
        places, across = shape
        _, all_places, shares, parts, side, _ = out_ref.shape
        size = rows * WINDOW
        first = (step - conv_steps) * places
        x = jnp.concatenate(
            [
                strided(acc_ref, share * across + part * all_places + first + j, size, strips)
                for j in range(places)
                for share in range(shares)
                for part in range(parts)
            ],
            axis=0,
        ).astype(jnp.bfloat16)
        result = attend_windows(x.astype(jnp.float32), block_gain_ref[...], wqkv_ref, wout_ref)
        result = result.astype(jnp.bfloat16).reshape(places, shares, parts, size // side, side, channels)
        for j in range(places):
            for share in range(shares):
                for part in range(parts):
                    out_ref[:, first + j, share, part] = result[j, share, part]


def conv_and_windows(moved, own, edges, ew0, ew1, gain, w_expand, dw_kernel, w_project, block_gain, w_qkv, w_out, rows, shape):
    tokens, channels = moved.shape
    cols = tokens // rows
    places, shares, parts = shape
    width = w_expand.shape[1]
    features = min(FEATURES, width)
    strips = cols // WINDOW
    conv_steps = width // features
    block_places = max(1, min(places, GROUP // (shares * parts)))
    side_rows = ew0.shape[0]
    side_count = side_rows + -side_rows % 16
    vmem = pl.BlockSpec(memory_space=pltpu.VMEM)
    return pl.pallas_call(
        functools.partial(conv_kernel, conv_steps, (block_places, strips // shares)),
        grid=(conv_steps + places // block_places,),
        out_shape=jax.ShapeDtypeStruct((rows, places, shares, parts, WINDOW, channels), jnp.bfloat16),
        in_specs=[
            *[vmem] * 5,
            vmem,
            vmem,
            pl.BlockSpec((3, 3, features), lambda step: (0, 0, jnp.minimum(step, conv_steps - 1))),
            vmem,
            vmem,
            vmem,
            vmem,
        ],
        out_specs=vmem,
        scratch_shapes=[
            pltpu.VMEM((2 * side_count, channels), jnp.bfloat16),
            pltpu.VMEM((rows + 2, WINDOW + 2, strips, features), jnp.bfloat16),
            pltpu.VMEM((channels // LANES, tokens + strips, LANES), jnp.float32),
        ],
        compiler_params=pltpu.CompilerParams(dimension_semantics=("arbitrary",), vmem_limit_bytes=CONV_LIMIT * MIB),
        cost_estimate=pl.CostEstimate(
            flops=4 * tokens * channels * (width + 4 * channels),
            bytes_accessed=4 * channels * (width + 2 * channels) + 4 * tokens * channels,
            transcendentals=2 * tokens * width,
        ),
        name="conv_and_windows",
    )(
        moved,
        own,
        edges,
        ew0,
        ew1,
        gain.reshape(1, channels),
        w_expand,
        dw_kernel,
        w_project,
        block_gain.reshape(1, channels),
        w_qkv,
        w_out,
    )


def attend_windows(x, gain, wqkv_ref, wout_ref):
    tokens, channels = x.shape
    head_dim = channels // HEADS
    group = LANES // head_dim
    size = WINDOW * WINDOW
    two = 2 * head_dim
    pairs, groups = tokens // (2 * size), channels // LANES
    units = [(p, g) for p in range(pairs) for g in range(groups)]
    scale = math.log2(math.e) / math.sqrt(head_dim)
    normed = normalize(x, gain).astype(jnp.bfloat16)

    def project(first):
        return jnp.dot(normed, wqkv_ref[:, first : first + channels], preferred_element_type=jnp.float32)

    queries = lax.dot_general(wqkv_ref[:, :channels].T, normed, NT, preferred_element_type=jnp.float32) * scale
    keys = project(channels).astype(jnp.bfloat16)
    values = lax.dot_general(
        wqkv_ref[:, 2 * channels :].T, normed, NT, preferred_element_type=jnp.float32
    ).astype(jnp.bfloat16)
    lane = lax.broadcasted_iota(jnp.int32, (1, LANES), 1)
    halves = [(lane // size == h).astype(jnp.float32).astype(jnp.bfloat16) for h in range(2)]
    scores = {}
    zeros = jnp.zeros((two, 2 * size), jnp.bfloat16)
    for p, g in units:
        own = queries[g * LANES : (g + 1) * LANES, p * 2 * size : (p + 1) * 2 * size]
        turned = pltpu.roll(own, size, axis=1).astype(jnp.bfloat16)
        own = own.astype(jnp.bfloat16)
        for odd in range(2):
            at = (2 * p + odd) * size
            k = keys[at : at + size, g * LANES : (g + 1) * LANES]
            columns = []
            for t in range(group // 2):
                heads = []
                for h in range(2):
                    source = own if h == odd else turned
                    row = t * two + h * head_dim
                    heads.append(source[row : row + head_dim] * halves[h])
                column = [zeros] * (group // 2)
                column[t] = jnp.concatenate(heads, axis=0)
                columns.append(jnp.concatenate(column, axis=0))
            scores[p, g, odd] = jnp.dot(k, jnp.concatenate(columns, axis=1), preferred_element_type=jnp.float32)
    weights = {}
    for unit, s in scores.items():
        raised = jnp.exp2(s - jnp.max(s, axis=0, keepdims=True))
        weights[unit] = (raised * (1.0 / jnp.sum(raised, axis=0, keepdims=True))).astype(jnp.bfloat16)
    mixed = {}
    for p, g in units:
        both = jnp.concatenate([weights[p, g, 0], weights[p, g, 1]], axis=0)
        for t in range(group // 2):
            at = g * LANES + t * two
            v = values[at : at + two, p * 2 * size : (p + 1) * 2 * size]
            v_halves = jnp.concatenate([v * m for m in halves], axis=0)
            mixed[p, g, t] = jnp.dot(
                v_halves, both[:, t * 2 * size : (t + 1) * 2 * size], preferred_element_type=jnp.float32
            )
    even_head = lane // head_dim % 2 == 0
    blended = []
    for p in range(pairs):
        for odd in range(2):
            parts = []
            for g in range(groups):
                turned = jnp.concatenate(
                    [mixed[p, g, t][odd * two : (odd + 1) * two] for t in range(group // 2)], axis=0
                ).T
                parts.append(jnp.where(even_head, turned[:size], turned[size:]).astype(jnp.bfloat16))
            blended.append(jnp.concatenate(parts, axis=1))
    return x + jnp.dot(jnp.concatenate(blended, axis=0), wout_ref[...], preferred_element_type=jnp.float32)


def grid_kernel(x_ref, gain_ref, wqkv_ref, wout_ref, out_ref, floats_ref):
    step = pl.program_id(0)
    tokens, channels = x_ref.shape
    size = WINDOW * WINDOW
    windows = tokens // size
    block = windows // pl.num_programs(0)

    @pl.when(step == 0)
    def _():
        for t, part in enumerate(tiles(x_ref[...])):
            floats_ref[t, :tokens] = part.astype(jnp.float32)

    first = step * block
    x = jnp.concatenate([strided(floats_ref, first + w, size, windows) for w in range(block)], axis=0)
    result = attend_windows(x, gain_ref[...], wqkv_ref, wout_ref)
    for t, part in enumerate(tiles(result)):
        for w in range(block):
            floats_ref[t, pl.ds(first + w, size, stride=windows), :] = part[w * size : (w + 1) * size]

    @pl.when(step == pl.num_programs(0) - 1)
    def _():
        for t in range(floats_ref.shape[0]):
            out_ref[:, t * LANES : (t + 1) * LANES] = floats_ref[t, :tokens].astype(jnp.bfloat16)


def grid_attention(x, gain, w_qkv, w_out):
    tokens, channels = x.shape
    windows = tokens // (WINDOW * WINDOW)
    vmem = pl.BlockSpec(memory_space=pltpu.VMEM)
    return pl.pallas_call(
        grid_kernel,
        grid=(windows // min(GROUP, windows),),
        out_shape=jax.ShapeDtypeStruct((tokens, channels), jnp.bfloat16),
        in_specs=[vmem] * 4,
        out_specs=vmem,
        scratch_shapes=[pltpu.VMEM((channels // LANES, tokens + windows, LANES), jnp.float32)],
        compiler_params=pltpu.CompilerParams(dimension_semantics=("arbitrary",), vmem_limit_bytes=24 * MIB),
        cost_estimate=pl.CostEstimate(
            flops=16 * tokens * channels * channels,
            bytes_accessed=8 * channels * channels + 4 * tokens * channels,
            transcendentals=HEADS * tokens * WINDOW * WINDOW,
        ),
        name="grid_attention",
    )(x, gain.reshape(1, channels), w_qkv, w_out)


def swap(low_edge, high_edge, axis, first):
    pairs = [(a, a + 1) for a in range(first, lax.axis_size(axis) - 1, 2)]
    lower = lax.rem(lax.axis_index(axis), 2) == first
    return lax.ppermute(
        jnp.where(lower, high_edge, low_edge), axis, pairs + [(target, source) for source, target in pairs]
    )


def swap_columns(tokens, corners0, corners1):
    even = lax.rem(lax.axis_index("ns"), 2) == 0

    def column(c, k):
        north, south = jnp.where(even, corners1[k], corners0[k]), jnp.where(even, corners0[k], corners1[k])
        return jnp.concatenate([north[None], tokens[:, c], south[None]])

    low, high = column(0, 0), column(tokens.shape[1] - 1, 1)
    return [swap(low, high, "ew", first) for first in range(2)]


def exchange(x):
    bands, strips = lax.axis_size("ns"), lax.axis_size("ew")
    if bands == WINDOW:
        return lax.all_to_all(x, ("ns", "ew"), 0, 0, tiled=True)
    inner = bands // WINDOW
    groups = [[a * inner + p for a in range(WINDOW)] for p in range(inner)]
    shape = x.shape
    x = x.reshape(WINDOW, strips, *shape[1:])
    x = lax.all_to_all(x, "ns", 0, 0, axis_index_groups=groups, tiled=True)
    x = lax.all_to_all(x, "ew", 1, 1, tiled=True)
    return x.reshape(shape)


def on_device(
    tokens,
    conv_gain,
    w_expand,
    dw_kernel,
    w_project,
    block_gain,
    block_qkv,
    block_out,
    grid_gain,
    grid_qkv,
    grid_out,
):
    rows, cols, channels = tokens.shape
    shares = WINDOW // lax.axis_size("ew")
    group = WINDOW * lax.axis_size("ew")
    across = cols // shares // WINDOW
    places = group // rows
    parts = across // places
    ns0, ns1 = [swap(tokens[0], tokens[rows - 1], "ns", first) for first in range(2)]
    own, moved = norm_own(tokens, conv_gain)
    corners = [jnp.concatenate([ns[:1], ns[cols - 1 :]]) for ns in (ns0, ns1)]
    corners, own, moved = lax.optimization_barrier((corners, own, moved))
    ew0, ew1 = swap_columns(tokens, *corners)
    sent = conv_and_windows(
        moved,
        own,
        expand_edges(ns0, ns1, conv_gain, w_expand),
        ew0,
        ew1,
        conv_gain,
        w_expand,
        dw_kernel,
        w_project,
        block_gain,
        block_qkv,
        block_out,
        rows,
        (places, shares, parts),
    )
    x = exchange(sent.reshape(group, -1, channels))
    y = grid_attention(x.reshape(-1, channels), grid_gain, grid_qkv, grid_out)
    returned = exchange(y.reshape(group, -1, channels)).reshape(rows, places, shares, parts, WINDOW, channels)
    return jnp.transpose(returned, (0, 2, 3, 1, 4, 5)).reshape(rows, cols, channels)


def solution(mesh):
    in_specs = (P("ns", "ew", None), P(), P(), P(), P(), P(), P(), P(), P(), P(), P())
    out_specs = P("ns", "ew", None)
    return jax.shard_map(
        on_device, mesh=mesh, in_specs=in_specs, out_specs=out_specs, check_vma=False
    )
```

```python
import functools
import math

import jax
import jax.numpy as jnp
from jax import lax
from jax.experimental import pallas as pl
from jax.experimental.pallas import tpu as pltpu
from jax.sharding import PartitionSpec as P

HEADS = 16
WINDOW = 8
FEATURES = 2048
LANES = 128
GROUP = 16
MIB = 1024 * 1024
NORM_LIMIT = 8
EDGE_LIMIT = 12
NORM_COST = 10_000_000_000
CONV_LIMIT = 32

NT = (((1,), (1,)), ((), ()))


def normalize(floats, scale_gain):
    center = floats - jnp.mean(floats, axis=-1, keepdims=True)
    spread = jnp.mean(center * center, axis=-1, keepdims=True)
    return center * lax.rsqrt(spread + 1e-05) * scale_gain


def gelu_of_double(half):
    root = math.sqrt(2 / math.pi)
    inner = half * (2 * root + (8 * root * 0.044715) * (half * half))
    return half + half * jnp.tanh(inner)


def tiles(value):
    return [value[:, t : t + LANES] for t in range(0, value.shape[1], LANES)]


def strided(ref, start, size, stride):
    return jnp.concatenate([ref[t, pl.ds(start, size, stride=stride), :] for t in range(ref.shape[0])], axis=1)


def by_place(tmp_ref, block, store):
    cols = block.shape[0]
    strips = cols // WINDOW
    for t, part in enumerate(tiles(block)):
        tmp_ref[t, :cols] = part
    for b in range(WINDOW):
        store(b * strips, strips, strided(tmp_ref, b, strips, WINDOW))


def norm_kernel(x_ref, gain_ref, normed_ref, moved_ref, tmp_ref):
    rows, cols, _ = x_ref.shape
    gain = 0.5 * gain_ref[...]
    for i in range(rows):

        block = x_ref[i].astype(jnp.float32)
        for out_ref, value in ((normed_ref, normalize(block, gain)), (moved_ref, block)):

            def store(at, count, part):
                out_ref[i * cols + at : i * cols + at + count, :] = part.astype(jnp.bfloat16)

            by_place(tmp_ref, value, store)


def norm_own(tokens, gain):
    rows, cols, channels = tokens.shape
    return pl.pallas_call(
        norm_kernel,
        out_shape=[jax.ShapeDtypeStruct((rows * cols, channels), jnp.bfloat16)] * 2,
        scratch_shapes=[pltpu.VMEM((channels // LANES, cols + WINDOW, LANES), jnp.float32)],
        compiler_params=pltpu.CompilerParams(vmem_limit_bytes=NORM_LIMIT * MIB),
        cost_estimate=pl.CostEstimate(flops=NORM_COST, bytes_accessed=4 * rows * cols * channels, transcendentals=0),
        name="norm_own",
    )(tokens, gain.reshape(1, channels))


def sorted_pair(first_ref, second_ref, axis):
    first, second = first_ref[...].astype(jnp.float32), second_ref[...].astype(jnp.float32)
    even = lax.rem(lax.axis_index(axis), 2) == 0
    return jnp.where(even, second, first), jnp.where(even, first, second)


def edge_kernel(ns0_ref, ns1_ref, gain_ref, w1_ref, out_ref, n_ref, tmp_ref):
    cols = ns0_ref.shape[0]
    gain = 0.5 * gain_ref[...]
    for k, block in enumerate(sorted_pair(ns0_ref, ns1_ref, "ns")):

        def store(at, count, part):
            n_ref[k * cols + at : k * cols + at + count, :] = part.astype(jnp.bfloat16)

        by_place(tmp_ref, normalize(block, gain), store)
    for k in range(2):
        normed = n_ref[k * cols : (k + 1) * cols, :]
        hidden = jnp.dot(normed, w1_ref[...], preferred_element_type=jnp.float32)
        out_ref[k] = gelu_of_double(hidden.astype(jnp.bfloat16)).reshape(out_ref.shape[1:])


def expand_edges(ns0, ns1, gain, w_expand):
    cols, channels = ns0.shape
    width = w_expand.shape[1]
    vmem = pl.BlockSpec(memory_space=pltpu.VMEM)
    return pl.pallas_call(
        edge_kernel,
        out_shape=jax.ShapeDtypeStruct((2, WINDOW, cols // WINDOW, width), jnp.bfloat16),
        in_specs=[vmem] * 4,
        out_specs=vmem,
        scratch_shapes=[
            pltpu.VMEM((2 * cols, channels), jnp.bfloat16),
            pltpu.VMEM((channels // LANES, cols + WINDOW, LANES), jnp.float32),
        ],
        compiler_params=pltpu.CompilerParams(vmem_limit_bytes=EDGE_LIMIT * MIB),
        cost_estimate=pl.CostEstimate(
            flops=4 * cols * channels * width,
            bytes_accessed=2 * channels * width + 4 * cols * (channels + width),
            transcendentals=2 * cols * width,
        ),
        name="expand_edges",
    )(ns0, ns1, gain.reshape(1, channels), w_expand)


def conv_kernel(
    conv_steps, shape, x_ref, own_ref, edge_ref, ew0_ref, ew1_ref, gain_ref, w1_ref, dw_ref, w2_ref,
    block_gain_ref, wqkv_ref, wout_ref, out_ref, n_ref, e_ref, acc_ref
):
    step = pl.program_id(0)
    tokens, channels = x_ref.shape
    rows = out_ref.shape[0]
    cols = tokens // rows
    strips = cols // WINDOW
    features = w1_ref.shape[1] // conv_steps
    side_rows = ew0_ref.shape[0]
    side_count = side_rows + -side_rows % 16

    @pl.when(step == 0)
    def _():
        gain = 0.5 * gain_ref[...]

        pad = jnp.zeros((side_count - side_rows, channels), jnp.float32)
        for k, block in enumerate(sorted_pair(ew0_ref, ew1_ref, "ew")):
            start = k * side_count
            n_ref[start : start + side_count, :] = normalize(
                jnp.concatenate([block, pad], axis=0), gain
            ).astype(jnp.bfloat16)
        if conv_steps > 1:
            for t in range(channels // LANES):
                acc_ref[t, :tokens] = x_ref[:, t * LANES : (t + 1) * LANES].astype(jnp.float32)

    @pl.when(step < conv_steps)
    def _():
        block = pl.ds(pl.multiple_of(step * features, features), features)
        w1 = w1_ref[:, block]
        w2 = w2_ref[block, :]
        taps = [[(0.5 * dw_ref[a, b : b + 1, :]).astype(jnp.bfloat16) for b in range(3)] for a in range(3)]

        def hidden(normed):
            return gelu_of_double(jnp.dot(normed, w1, preferred_element_type=jnp.float32).astype(jnp.bfloat16))

        sides = hidden(n_ref[...]).astype(jnp.float32)
        place_in_strip = lax.broadcasted_iota(jnp.int32, (strips, features), 0)
        for i in range(rows + 2):
            if i in (0, rows + 1):
                own = edge_ref[i // (rows + 1), :, :, block]
            else:
                own = hidden(own_ref[(i - 1) * cols : i * cols, :]).reshape(WINDOW, strips, features)
            e_ref[i, 1 : WINDOW + 1] = own
            last = pltpu.roll(own[WINDOW - 1].astype(jnp.float32), 1, axis=0)
            first = pltpu.roll(own[0].astype(jnp.float32), strips - 1, axis=0)
            low = jnp.where(place_in_strip == 0, sides[i : i + 1], last)
            high = jnp.where(place_in_strip == strips - 1, sides[side_count + i : side_count + i + 1], first)
            e_ref[i, 0] = low.astype(jnp.bfloat16)
            e_ref[i, WINDOW + 1] = high.astype(jnp.bfloat16)
        for i in range(rows):
            pieces = []
            for b in range(WINDOW):
                sums = []
                for da in range(3):
                    t = [e_ref[i + da, b + db] * taps[da][db] for db in range(3)]
                    sums.append(t[0] + t[1] + t[2])
                pieces.append(gelu_of_double(sums[0] + sums[1] + sums[2]))
            active = jnp.concatenate(pieces, axis=0)
            for t, part in enumerate(tiles(jnp.dot(active, w2, preferred_element_type=jnp.float32))):
                own_rows = slice(i * cols, (i + 1) * cols)
                if conv_steps > 1:
                    acc_ref[t, own_rows, :] += part
                else:
                    acc_ref[t, own_rows, :] = (
                        x_ref[own_rows, t * LANES : (t + 1) * LANES].astype(jnp.float32) + part
                    )

    @pl.when(step >= conv_steps)
    def _():
        places, across = shape
        _, all_places, shares, parts, side, _ = out_ref.shape
        size = rows * WINDOW
        first = (step - conv_steps) * places
        x = jnp.concatenate(
            [
                strided(acc_ref, share * across + part * all_places + first + j, size, strips)
                for j in range(places)
                for share in range(shares)
                for part in range(parts)
            ],
            axis=0,
        ).astype(jnp.bfloat16)
        result = attend_windows(x.astype(jnp.float32), block_gain_ref[...], wqkv_ref, wout_ref)
        result = result.astype(jnp.bfloat16).reshape(places, shares, parts, size // side, side, channels)
        for j in range(places):
            for share in range(shares):
                for part in range(parts):
                    out_ref[:, first + j, share, part] = result[j, share, part]


def conv_and_windows(moved, own, edges, ew0, ew1, gain, w_expand, dw_kernel, w_project, block_gain, w_qkv, w_out, rows, shape):
    tokens, channels = moved.shape
    cols = tokens // rows
    places, shares, parts = shape
    width = w_expand.shape[1]
    features = min(FEATURES, width)
    strips = cols // WINDOW
    conv_steps = width // features
    block_places = max(1, min(places, GROUP // (shares * parts)))
    side_rows = ew0.shape[0]
    side_count = side_rows + -side_rows % 16
    vmem = pl.BlockSpec(memory_space=pltpu.VMEM)
    return pl.pallas_call(
        functools.partial(conv_kernel, conv_steps, (block_places, strips // shares)),
        grid=(conv_steps + places // block_places,),
        out_shape=jax.ShapeDtypeStruct((rows, places, shares, parts, WINDOW, channels), jnp.bfloat16),
        in_specs=[
            *[vmem] * 5,
            vmem,
            vmem,
            pl.BlockSpec((3, 3, features), lambda step: (0, 0, jnp.minimum(step, conv_steps - 1))),
            vmem,
            vmem,
            vmem,
            vmem,
        ],
        out_specs=vmem,
        scratch_shapes=[
            pltpu.VMEM((2 * side_count, channels), jnp.bfloat16),
            pltpu.VMEM((rows + 2, WINDOW + 2, strips, features), jnp.bfloat16),
            pltpu.VMEM((channels // LANES, tokens + strips, LANES), jnp.float32),
        ],
        compiler_params=pltpu.CompilerParams(dimension_semantics=("arbitrary",), vmem_limit_bytes=CONV_LIMIT * MIB),
        cost_estimate=pl.CostEstimate(
            flops=4 * tokens * channels * (width + 4 * channels),
            bytes_accessed=4 * channels * (width + 2 * channels) + 4 * tokens * channels,
            transcendentals=2 * tokens * width,
        ),
        name="conv_and_windows",
    )(
        moved,
        own,
        edges,
        ew0,
        ew1,
        gain.reshape(1, channels),
        w_expand,
        dw_kernel,
        w_project,
        block_gain.reshape(1, channels),
        w_qkv,
        w_out,
    )


def attend_windows(x, gain, wqkv_ref, wout_ref):
    tokens, channels = x.shape
    head_dim = channels // HEADS
    group = LANES // head_dim
    size = WINDOW * WINDOW
    two = 2 * head_dim
    pairs, groups = tokens // (2 * size), channels // LANES
    units = [(p, g) for p in range(pairs) for g in range(groups)]
    scale = math.log2(math.e) / math.sqrt(head_dim)
    normed = normalize(x, gain).astype(jnp.bfloat16)

    def project(first):
        return jnp.dot(normed, wqkv_ref[:, first : first + channels], preferred_element_type=jnp.float32)

    queries = lax.dot_general(wqkv_ref[:, :channels].T, normed, NT, preferred_element_type=jnp.float32) * scale
    keys = project(channels).astype(jnp.bfloat16)
    values = lax.dot_general(
        wqkv_ref[:, 2 * channels :].T, normed, NT, preferred_element_type=jnp.float32
    ).astype(jnp.bfloat16)
    lane = lax.broadcasted_iota(jnp.int32, (1, LANES), 1)
    halves = [(lane // size == h).astype(jnp.float32).astype(jnp.bfloat16) for h in range(2)]
    scores = {}
    zeros = jnp.zeros((two, 2 * size), jnp.bfloat16)
    for p, g in units:
        own = queries[g * LANES : (g + 1) * LANES, p * 2 * size : (p + 1) * 2 * size]
        turned = pltpu.roll(own, size, axis=1).astype(jnp.bfloat16)
        own = own.astype(jnp.bfloat16)
        for odd in range(2):
            at = (2 * p + odd) * size
            k = keys[at : at + size, g * LANES : (g + 1) * LANES]
            columns = []
            for t in range(group // 2):
                heads = []
                for h in range(2):
                    source = own if h == odd else turned
                    row = t * two + h * head_dim
                    heads.append(source[row : row + head_dim] * halves[h])
                column = [zeros] * (group // 2)
                column[t] = jnp.concatenate(heads, axis=0)
                columns.append(jnp.concatenate(column, axis=0))
            scores[p, g, odd] = jnp.dot(k, jnp.concatenate(columns, axis=1), preferred_element_type=jnp.float32)
    weights = {}
    for unit, s in scores.items():
        raised = jnp.exp2(s - jnp.max(s, axis=0, keepdims=True))
        weights[unit] = (raised * (1.0 / jnp.sum(raised, axis=0, keepdims=True))).astype(jnp.bfloat16)
    mixed = {}
    for p, g in units:
        both = jnp.concatenate([weights[p, g, 0], weights[p, g, 1]], axis=0)
        for t in range(group // 2):
            at = g * LANES + t * two
            v = values[at : at + two, p * 2 * size : (p + 1) * 2 * size]
            v_halves = jnp.concatenate([v * m for m in halves], axis=0)
            mixed[p, g, t] = jnp.dot(
                v_halves, both[:, t * 2 * size : (t + 1) * 2 * size], preferred_element_type=jnp.float32
            )
    even_head = lane // head_dim % 2 == 0
    blended = []
    for p in range(pairs):
        for odd in range(2):
            parts = []
            for g in range(groups):
                turned = jnp.concatenate(
                    [mixed[p, g, t][odd * two : (odd + 1) * two] for t in range(group // 2)], axis=0
                ).T
                parts.append(jnp.where(even_head, turned[:size], turned[size:]).astype(jnp.bfloat16))
            blended.append(jnp.concatenate(parts, axis=1))
    return x + jnp.dot(jnp.concatenate(blended, axis=0), wout_ref[...], preferred_element_type=jnp.float32)


def grid_kernel(x_ref, gain_ref, wqkv_ref, wout_ref, out_ref, floats_ref):
    step = pl.program_id(0)
    tokens, channels = x_ref.shape
    size = WINDOW * WINDOW
    windows = tokens // size
    block = windows // pl.num_programs(0)

    @pl.when(step == 0)
    def _():
        for t, part in enumerate(tiles(x_ref[...])):
            floats_ref[t, :tokens] = part.astype(jnp.float32)

    first = step * block
    x = jnp.concatenate([strided(floats_ref, first + w, size, windows) for w in range(block)], axis=0)
    result = attend_windows(x, gain_ref[...], wqkv_ref, wout_ref)
    for t, part in enumerate(tiles(result)):
        for w in range(block):
            floats_ref[t, pl.ds(first + w, size, stride=windows), :] = part[w * size : (w + 1) * size]

    @pl.when(step == pl.num_programs(0) - 1)
    def _():
        for t in range(floats_ref.shape[0]):
            out_ref[:, t * LANES : (t + 1) * LANES] = floats_ref[t, :tokens].astype(jnp.bfloat16)


def grid_attention(x, gain, w_qkv, w_out):
    tokens, channels = x.shape
    windows = tokens // (WINDOW * WINDOW)
    vmem = pl.BlockSpec(memory_space=pltpu.VMEM)
    return pl.pallas_call(
        grid_kernel,
        grid=(windows // min(GROUP, windows),),
        out_shape=jax.ShapeDtypeStruct((tokens, channels), jnp.bfloat16),
        in_specs=[vmem] * 4,
        out_specs=vmem,
        scratch_shapes=[pltpu.VMEM((channels // LANES, tokens + windows, LANES), jnp.float32)],
        compiler_params=pltpu.CompilerParams(dimension_semantics=("arbitrary",), vmem_limit_bytes=24 * MIB),
        cost_estimate=pl.CostEstimate(
            flops=16 * tokens * channels * channels,
            bytes_accessed=8 * channels * channels + 4 * tokens * channels,
            transcendentals=HEADS * tokens * WINDOW * WINDOW,
        ),
        name="grid_attention",
    )(x, gain.reshape(1, channels), w_qkv, w_out)


def swap(low_edge, high_edge, axis, first):
    pairs = [(a, a + 1) for a in range(first, lax.axis_size(axis) - 1, 2)]
    lower = lax.rem(lax.axis_index(axis), 2) == first
    return lax.ppermute(
        jnp.where(lower, high_edge, low_edge), axis, pairs + [(target, source) for source, target in pairs]
    )


def swap_columns(tokens, corners0, corners1):
    even = lax.rem(lax.axis_index("ns"), 2) == 0

    def column(c, k):
        north, south = jnp.where(even, corners1[k], corners0[k]), jnp.where(even, corners0[k], corners1[k])
        return jnp.concatenate([north[None], tokens[:, c], south[None]])

    low, high = column(0, 0), column(tokens.shape[1] - 1, 1)
    return [swap(low, high, "ew", first) for first in range(2)]


def exchange(x):
    bands, strips = lax.axis_size("ns"), lax.axis_size("ew")
    if bands == WINDOW:
        return lax.all_to_all(x, ("ns", "ew"), 0, 0, tiled=True)
    inner = bands // WINDOW
    groups = [[a * inner + p for a in range(WINDOW)] for p in range(inner)]
    shape = x.shape
    x = x.reshape(WINDOW, strips, *shape[1:])
    x = lax.all_to_all(x, "ns", 0, 0, axis_index_groups=groups, tiled=True)
    x = lax.all_to_all(x, "ew", 1, 1, tiled=True)
    return x.reshape(shape)


def on_device(
    tokens,
    conv_gain,
    w_expand,
    dw_kernel,
    w_project,
    block_gain,
    block_qkv,
    block_out,
    grid_gain,
    grid_qkv,
    grid_out,
):
    rows, cols, channels = tokens.shape
    shares = WINDOW // lax.axis_size("ew")
    group = WINDOW * lax.axis_size("ew")
    across = cols // shares // WINDOW
    places = group // rows
    parts = across // places
    ns0, ns1 = [swap(tokens[0], tokens[rows - 1], "ns", first) for first in range(2)]
    own, moved = norm_own(tokens, conv_gain)
    corners = [jnp.concatenate([ns[:1], ns[cols - 1 :]]) for ns in (ns0, ns1)]
    corners, own, moved = lax.optimization_barrier((corners, own, moved))
    ew0, ew1 = swap_columns(tokens, *corners)
    sent = conv_and_windows(
        moved,
        own,
        expand_edges(ns0, ns1, conv_gain, w_expand),
        ew0,
        ew1,
        conv_gain,
        w_expand,
        dw_kernel,
        w_project,
        block_gain,
        block_qkv,
        block_out,
        rows,
        (places, shares, parts),
    )
    x = exchange(sent.reshape(group, -1, channels))
    y = grid_attention(x.reshape(-1, channels), grid_gain, grid_qkv, grid_out)
    returned = exchange(y.reshape(group, -1, channels)).reshape(rows, places, shares, parts, WINDOW, channels)
    return jnp.transpose(returned, (0, 2, 3, 1, 4, 5)).reshape(rows, cols, channels)


def solution(mesh):
    in_specs = (P("ns", "ew", None), P(), P(), P(), P(), P(), P(), P(), P(), P(), P())
    out_specs = P("ns", "ew", None)
    return jax.shard_map(
        on_device, mesh=mesh, in_specs=in_specs, out_specs=out_specs, check_vma=False
    )
```
